32 devices in a mesh: peer: 2 (over x), depth: 4 (over z), row: 4 (over y, core).
Axes of the slice: x: 2, y: 2, z: 4, core: 2. Of those that a mesh axis runs over, the one named last changes fastest.
Arguments:
- features: bfloat16 [12, 32, 2048], P('depth', 'row'), may hold values from -6 to 6
- labels: int32 [12, 32, 64], P('depth', 'row'), may hold values from 0 to 103
- conv_weights: bfloat16 [2, 4, 864, 32], P('peer'), may hold values from -0.21875 to 0.21875
- head_weights: bfloat16 [2, 32, 104], P('peer'), may hold values from -4 to 4
- matching: int32 [12, 2], P('depth'), may hold values from 0 to 1, each once within a row
Outputs:
- conv_grads: float32 [2, 4, 864, 32], P('peer')
- head_grads: float32 [2, 32, 104], P('peer')
- input_grads: bfloat16 [2, 12, 32, 2048], P('peer', 'depth', 'row')
The draws below stay inside these ranges and needn't reach their ends.
Inputs may be any that keep to these rules, and one draw needn't show every extreme that they name: `matching`: in every depth plane every peer is distilled by exactly one peer.
All inputs are finite; a program needn't handle non-finite values.
Results may differ from the reference program's by a relative error of at most 0.019.
Values may be sent and summed in bfloat16 or wider, within the bound.
No kernel may reach another device: no remote copies, remote signals or barrier semaphores. Data moves between devices by JAX's collectives and lax.ppermute only.
A program may use at most 64 MiB of HBM per device.

```python
import jax
import jax.numpy as jnp
from jax import lax

C = 32
K = 104
LAYERS = 4
WIDTH = 64
PEERS = 2
DEPTH = 12
ROWS = 32
N_PEER = 2


def with_ends(array, own_key, low, largest):
    index_at = [jax.random.randint(jax.random.fold_in(own_key, axis), (), 0, length) for axis, length in enumerate(array.shape)]
    main_axis = array.shape.index(max(array.shape))
    beside = index_at[:main_axis] + [(index_at[main_axis] + 1) % array.shape[main_axis]] + index_at[main_axis + 1:]
    return array.at[tuple(index_at)].set(low).at[tuple(beside)].set(largest)


def block_levels(stream_key, dims, cuts, least, largest):
    def one(dim, blocks):
        steps = jax.random.uniform(jax.random.fold_in(jax.random.fold_in(stream_key, 6), dim), (blocks,), jnp.float32, least / len(cuts), largest / len(cuts))
        return jnp.repeat(jnp.exp(steps), dims[dim] // blocks).reshape((-1,) + (1,) * (len(dims) - dim - 1))

    loudness = one(*cuts[0])
    for cut in cuts[1:]:
        loudness = loudness * one(*cut)
    return loudness


def noise(own_key, extent, width, limit, split=(), kind=jnp.bfloat16):
    values = jax.random.normal(own_key, extent, jnp.float32) * width
    if len(split) > 0:
        values = block_levels(own_key, extent, split, -0.22, 0.18) * values
    return jnp.clip(values, min=-limit, max=limit).astype(kind)


def setup_inputs(seed: int = 0) -> dict:
    seeds = jax.random.split(jax.random.key(seed), 6)
    features = noise(seeds[0], (DEPTH, ROWS, WIDTH * C), 1.0, 6.0, ((0, 4), (1, 4)))
    labels = with_ends(jax.random.randint(seeds[1], (DEPTH, ROWS, WIDTH), 0, K), jax.random.fold_in(seeds[1], 1), 0, K - 1).astype(jnp.int32)
    conv_weights = noise(seeds[2], (PEERS, LAYERS, 27 * C, C), (27 * C) ** -0.5, 0.21875, ((0, 2),))
    head_weights = noise(seeds[3], (PEERS, C, K), (C // 16) ** -0.5, 4.0, ((0, 2),))
    matching = jax.vmap(lambda own: jax.random.permutation(own, PEERS))(jax.random.split(seeds[4], DEPTH)).reshape((DEPTH, PEERS)).astype(jnp.int32)
    return {"features": features, "labels": labels, "conv_weights": conv_weights, "head_weights": head_weights, "matching": matching}


def columns(block, rows_out, width_out):
    pieces = []
    for depth_off in range(3):
        for row_off in range(3):
            for col_off in range(3):
                pieces.append(block[depth_off, row_off:row_off + rows_out, col_off:col_off + width_out, :])
    return jnp.concatenate(pieces, axis=-1).reshape(rows_out * width_out, -1)

def widened(padded, channels):
    depth_in, rows_in, merged = padded.shape
    volume = padded.reshape(depth_in, rows_in, merged // channels, channels)
    return jnp.pad(volume, ((0, 0), (0, 0), (1, 1), (0, 0)))

def convolve(padded, weight):
    channels = weight.shape[1]
    volume = widened(padded, channels)
    depth_out = padded.shape[0] - 2
    rows_out = padded.shape[1] - 2
    width_out = volume.shape[2] - 2
    weight_wide = weight.astype(jnp.float32)

    def one_slice(depth_index):
        block = lax.dynamic_slice_in_dim(volume, depth_index, 3, 0)
        cols = columns(block, rows_out, width_out).astype(jnp.float32)
        return jnp.dot(cols, weight_wide, precision=lax.Precision.HIGHEST)
    result = lax.map(one_slice, jnp.arange(depth_out, dtype=jnp.int32))
    return result.reshape(depth_out, rows_out, width_out * channels)

def weight_grad(padded, grad_out, channels):
    volume = widened(padded, channels)
    depth_out = padded.shape[0] - 2
    rows_out = padded.shape[1] - 2
    width_out = volume.shape[2] - 2
    grads = grad_out.reshape(depth_out, rows_out * width_out, channels)

    def accumulate(carry, depth_index):
        block = lax.dynamic_slice_in_dim(volume, depth_index, 3, 0)
        cols = columns(block, rows_out, width_out).astype(jnp.float32)
        slab = lax.dynamic_index_in_dim(grads, depth_index, 0, keepdims=False).astype(jnp.float32)
        return (carry + jnp.dot(cols.T, slab, precision=lax.Precision.HIGHEST), None)
    init = jnp.zeros((27 * channels, channels), jnp.float32)
    result, unused = lax.scan(accumulate, init, jnp.arange(depth_out, dtype=jnp.int32))
    return result

def flipped(weight):
    channels = weight.shape[1]
    return weight.reshape(27, channels, channels)[::-1].transpose(0, 2, 1).reshape(27 * channels, channels)

def padding(volume):
    return jnp.pad(volume, ((1, 1), (1, 1), (0, 0)))

def slope(pre):
    value = pre.astype(jnp.float32)
    sigma = jax.nn.sigmoid(value)
    return sigma * (1.0 + value * (1.0 - sigma))

def forward(features, kernels, head):
    layers = kernels.shape[0]
    current = features
    padded_list = []
    pre_list = []
    activations = [features]
    for layer in range(layers):
        padded = padding(current)
        padded_list.append(padded)
        pre_full = convolve(padded, kernels[layer])
        pre_list.append(pre_full.astype(jnp.bfloat16))
        current = jax.nn.silu(pre_full).astype(jnp.bfloat16)
        activations.append(current)
    channels = kernels.shape[2]
    hidden = current.reshape(-1, channels)
    logits = jnp.dot(hidden.astype(jnp.float32), head.astype(jnp.float32), precision=lax.Precision.HIGHEST)
    exponent = jnp.exp(logits)
    probs = exponent / lax.optimization_barrier(jnp.sum(exponent, axis=1, keepdims=True))
    return (padded_list, pre_list, hidden, probs)

def reference(features, labels, conv_weights, head_weights, matching):
    channels = conv_weights.shape[3]
    classes = head_weights.shape[2]
    layers = conv_weights.shape[1]
    depth_all, rows_all, merged = features.shape
    voxels = labels.size
    onehot = (labels.reshape(voxels, 1) == jnp.arange(classes, dtype=jnp.int32)[None, :]).astype(jnp.float32)

    def shared_of(peer):
        return forward(features, conv_weights[peer], head_weights[peer])[3].astype(jnp.bfloat16)
    all_shared = lax.map(shared_of, jnp.arange(N_PEER, dtype=jnp.int32))
    all_shared = all_shared.reshape(N_PEER, depth_all, voxels // depth_all, classes)

    def one_peer(peer):
        column = lax.dynamic_index_in_dim(matching, peer, 1, keepdims=False)

        def add(carry, source):
            piece = lax.dynamic_index_in_dim(all_shared, source, 0, keepdims=False).astype(jnp.float32)
            chosen = (column == source).astype(jnp.float32)
            return (carry + chosen[:, None, None] * piece, None)
        start = jnp.zeros((depth_all, voxels // depth_all, classes), jnp.float32)
        partner_shared, unused = lax.scan(add, start, jnp.arange(N_PEER, dtype=jnp.int32))
        partner_shared = partner_shared.reshape(voxels, classes)
        padded_list, pre_list, hidden, probs = forward(features, conv_weights[peer], head_weights[peer])
        mixed_grad = probs - 0.5 * onehot - 0.5 * partner_shared
        head_part = jnp.dot(hidden.astype(jnp.float32).T, mixed_grad, precision=lax.Precision.HIGHEST)
        back_hidden = jnp.dot(mixed_grad, head_weights[peer].astype(jnp.float32).T, precision=lax.Precision.HIGHEST)
        last_slope = slope(pre_list[layers - 1]).reshape(voxels, channels)
        grad_pre = (back_hidden * last_slope).astype(jnp.bfloat16).reshape(depth_all, rows_all, merged)
        kernel_grads = [None] * layers
        input_grad = None
        for layer in reversed(range(layers)):
            kernel_grads[layer] = weight_grad(padded_list[layer], grad_pre, channels)
            back_input = convolve(padding(grad_pre), flipped(conv_weights[peer, layer]))
            if layer > 0:
                grad_pre = (back_input * slope(pre_list[layer - 1])).astype(jnp.bfloat16)
            else:
                input_grad = back_input.astype(jnp.bfloat16)
        return (jnp.stack(kernel_grads), head_part, input_grad)
    return lax.map(one_peer, jnp.arange(N_PEER, dtype=jnp.int32))
```

```python
import functools

import jax
import jax.numpy as jnp
from jax import lax
from jax.experimental import pallas as pl
from jax.experimental.pallas import tpu as pltpu
from jax.sharding import PartitionSpec as P

HALO = 8
LANES = 128
F32 = jnp.float32
BF16 = jnp.bfloat16
GROUP = ("depth", "row")


def round_up(value, step):
    return -(-value // step) * step


class Plan:
    def __init__(self, mesh, features, labels, conv_weights, head_weights):
        self.n_depth = mesh.shape["depth"]
        self.n_row = mesh.shape["row"]
        self.n_peer = mesh.shape["peer"]
        self.n = self.n_depth * self.n_row
        self.slab_depth, self.slab_rows, merged = features.shape
        self.layers, self.taps, self.channels = conv_weights.shape[1:]
        self.classes = head_weights.shape[2]
        self.width = merged // self.channels
        self.depth = self.slab_depth * self.n_depth
        self.rows = self.slab_rows * self.n_row
        self.m = self.depth * self.rows
        self.slab = self.slab_depth * self.slab_rows
        self.own = self.width // self.n
        self.span = 2 * LANES // self.channels
        self.group = LANES // self.channels
        self.blocks = round_up(2 * HALO + self.own, self.group) // self.group
        self.window = self.blocks * self.group
        self.tile = 2 * LANES
        self.lane_blocks = round_up(self.taps, LANES) // LANES
        self.grad_rows = (self.layers * self.lane_blocks + 1) * self.channels
        self.chunk = round_up(-(-self.grad_rows // self.n), 8)
        self.back_rows = round_up(self.chunk + self.slab, 8)


def starts(low, high, span):
    found = []
    at = low
    while True:
        found.append(max(min(at, high - span), 0))
        if at + span >= high:
            return found
        at += span - 2


def lane_voxel(start, span, channels, lanes):
    residue = lax.broadcasted_iota(jnp.int32, (1, lanes), 1) // channels
    return start + lax.rem(residue - start % span + span, span)


def gather_tile(start, sources, load, plan, lanes=None):
    span, channels = plan.span, plan.channels
    lanes = lanes or plan.tile
    voxel = lane_voxel(start, span, channels, plan.tile)[:, :lanes]
    count = lanes // channels
    wanted = [start + (r - start) % span for r in range(count)]
    picks = []
    for v in wanted:
        picks.append(next((n for n, (lo, hi) in enumerate(sources) if lo <= v < hi), None))
    used = [n for n in dict.fromkeys(picks) if n is not None]
    value = load(used[0])
    for n in used[1:]:
        lows = [v for v, p in zip(wanted, picks) if p == n]
        mask = (voxel >= min(lows)) & (voxel <= max(lows))
        value = jnp.where(mask, load(n), value)
    return value


def crop_mask(voxel, base, plan):
    place = voxel + base
    return (place >= 0) & (place < plan.width)


def position(plan):
    return lax.axis_index("depth") * plan.n_row + lax.axis_index("row")


def store_shifted(xs, slot, value, plan):
    m, rows = plan.m, plan.rows
    row = lax.rem(lax.broadcasted_iota(jnp.int32, (m, 1), 0), rows)
    body = pl.ds(rows, m)
    xs[slot, 1, body, :] = value.astype(BF16)
    xs[slot, 0, body, :] = jnp.where(row == 0, 0.0, pltpu.roll(value, 1, 0)).astype(BF16)
    xs[slot, 2, body, :] = jnp.where(row == rows - 1, 0.0, pltpu.roll(value, m - 1, 0)).astype(BF16)


def clear_edges(xs, slots, plan):
    rows = plan.rows
    zero = jnp.zeros((rows, plan.tile), BF16)
    for slot in range(slots):
        for j in range(3):
            xs[slot, j, 0:rows, :] = zero
            xs[slot, j, rows + plan.m : 2 * rows + plan.m, :] = zero


def build_bands(weights_ref, band, plan):
    ch, span, tile = plan.channels, plan.span, plan.tile
    eye_r = lax.broadcasted_iota(jnp.int32, (ch, tile), 0)
    eye_l = lax.broadcasted_iota(jnp.int32, (ch, tile), 1)
    spread = (eye_r == lax.rem(eye_l, ch)).astype(BF16)
    block = eye_l // ch
    masks = [(block == b).astype(BF16) for b in range(span)]

    def one(step, carry):
        layer = step // 9
        ij = lax.rem(step, 9)
        part = weights_ref[0, layer, pl.ds(pl.multiple_of(ij * 3 * ch, 3 * ch), 3 * ch), :]
        wide = jnp.dot(part, spread, preferred_element_type=F32).astype(BF16)
        for a in range(span):
            rows = (
                wide[0:ch] * masks[(a + 1) % span]
                + wide[ch : 2 * ch] * masks[a]
                + wide[2 * ch : 3 * ch] * masks[(a - 1) % span]
            )
            band[layer, pl.ds(pl.multiple_of(ij * tile + a * ch, ch), ch), :] = rows
        return carry

    lax.fori_loop(0, plan.layers * 9, one, 0)


def head_matrix(head, plan):
    ch, group = plan.channels, plan.group
    lanes = lax.broadcasted_iota(jnp.int32, (ch, group * LANES), 1) // LANES
    wide = jnp.concatenate([head] * group, axis=1)
    zero = jnp.zeros_like(wide)
    return jnp.concatenate([jnp.where(lanes == v, wide, zero) for v in range(group)], axis=0)


def pack_kernel(plan, match_ref, feat_ref, label_ref, out_ref):
    ch, own = plan.channels, plan.own
    feats = feat_ref[...].astype(F32).reshape(plan.slab, plan.width * ch)
    labels = label_ref[...].astype(F32)
    peer = lax.axis_index("peer")
    lane = lax.broadcasted_iota(jnp.int32, (plan.slab_rows, LANES), 1)
    seen = 3 * plan.group
    matches = jnp.zeros((plan.slab_rows, LANES), F32)
    for k in range(plan.slab_depth):
        matches = jnp.where(lane == LANES - plan.slab_depth + k, match_ref[k, peer].astype(F32), matches)

    def cut(array, low, high, limit):
        pieces = []
        if low < 0:
            pieces.append(jnp.zeros((array.shape[0], min(-low, high - low)), F32))
        if max(low, 0) < min(high, limit):
            pieces.append(array[:, max(low, 0) : min(high, limit)])
        if high > limit:
            pieces.append(jnp.zeros((array.shape[0], min(high - limit, high - low)), F32))
        return jnp.concatenate(pieces, axis=1) if len(pieces) > 1 else pieces[0]

    for p in range(plan.n):
        first = p * own - HALO
        parts = []
        for q in range(plan.blocks):
            low = (first + q * plan.group) * ch
            parts.append(cut(feats, low, low + LANES, plan.width * ch))
        low = p * own - plan.group
        pieces = []
        for k in range(plan.slab_depth):
            pieces.append(cut(labels[k], low, low + seen, plan.width))
        pieces.append(jnp.zeros((plan.slab_rows, LANES - plan.slab_depth * seen), F32))
        parts.append(jnp.concatenate(pieces, axis=1) + matches)
        out_ref[p] = jnp.concatenate(parts, axis=0).astype(BF16)


def forward_kernel(plan, recv_ref, weights_ref, head_ref, msg_ref, pre4_ref, label_ref, act_ref, pre_ref, band, xs, src, out):
    ch, span, tile, m, rows = plan.channels, plan.span, plan.tile, plan.m, plan.rows
    base = position(plan) * plan.own - HALO
    build_bands(weights_ref, band, plan)
    clear_edges(xs, 3, plan)

    n_blocks = round_up(plan.blocks, 2)
    for d in range(plan.n_depth):
        parts = [recv_ref[d * plan.n_row + r].astype(F32) for r in range(plan.n_row)]
        for k in range(plan.slab_depth):
            at = (d * plan.slab_depth + k) * rows
            for q in range(plan.blocks):
                low = q * plan.slab + k * plan.slab_rows
                piece = jnp.concatenate([x[low : low + plan.slab_rows] for x in parts], axis=0)
                src[q // 2, at : at + rows, (q % 2) * LANES : (q % 2 + 1) * LANES] = piece
            for q in range(plan.blocks, n_blocks):
                src[q // 2, at : at + rows, (q % 2) * LANES : (q % 2 + 1) * LANES] = jnp.zeros((rows, LANES), F32)
            low = plan.blocks * plan.slab
            piece = jnp.concatenate([x[low : low + plan.slab_rows] for x in parts], axis=0)
            seen = 3 * plan.group
            if k > 0:
                lane = lax.broadcasted_iota(jnp.int32, (1, LANES), 1)
                moved = pltpu.roll(piece, LANES - k * seen, 1)
                piece = jnp.where(lane < seen, moved, pltpu.roll(piece, LANES - k, 1))
            keep = LANES - plan.slab_depth
            lane = lax.broadcasted_iota(jnp.int32, (1, LANES), 1)
            label_ref[at : at + rows, :] = jnp.where(
                (lane < seen) | (lane == keep), piece, 0.0
            )

    sources = [(q * span, min((q + 1) * span, plan.window)) for q in range(n_blocks // 2)]
    low, high = 0, plan.window
    pre_slot = 0
    for layer in range(plan.layers):
        begin = starts(low, high, span)
        for t, s in enumerate(begin):
            store_shifted(xs, t, gather_tile(s, sources, lambda n: src[n], plan), plan)
        act_ref[layer] = gather_tile(HALO - 2, sources, lambda n: src[n], plan).astype(BF16)

        def one(t, carry, low=low, high=high, layer=layer):
            total = jnp.dot(xs[t, 0, 0:m, :], band[layer, 0:tile, :], preferred_element_type=F32)
            for ij in range(1, 9):
                i, j = divmod(ij, 3)
                total = total + jnp.dot(
                    xs[t, j, i * rows : i * rows + m, :],
                    band[layer, ij * tile : (ij + 1) * tile, :],
                    preferred_element_type=F32,
                )
            out[t] = total
            begin_t = jnp.maximum(jnp.minimum(low + t * (span - 2), high - span), 0)
            voxel = begin_t + lax.rem(
                lax.broadcasted_iota(jnp.int32, (1, tile), 1) // ch - lax.rem(begin_t, span) + span, span
            )
            value = total / (1.0 + jnp.exp(-total))
            src[t] = jnp.where(crop_mask(voxel, base, plan), value, 0.0).astype(BF16).astype(F32)
            return carry

        lax.fori_loop(0, len(begin), one, 0)
        sources = [(s + 1, s + span - 1) for s in begin]
        low, high = low + 1, high - 1
        if layer < plan.layers - 1:
            for s in backward_starts(plan)[plan.layers - 2 - layer]:
                pre_ref[pre_slot] = gather_tile(s, sources, lambda n: out[n], plan).astype(BF16)
                pre_slot += 1
    for g in range(3):
        first = HALO + (g - 1) * plan.group
        half = slice(LANES, tile) if (first % span) else slice(0, LANES)
        whole = first - first % span
        cols = slice(g * LANES, (g + 1) * LANES)
        msg_ref[0:m, cols] = half_tile(whole, half, sources, src, plan).astype(BF16)
        pre4_ref[:, cols] = half_tile(whole, half, sources, out, plan).astype(BF16)
    msg_ref[m : m + ch, 0:LANES] = head_ref[...]
    msg_ref[m : m + ch, LANES : 3 * LANES] = jnp.zeros((ch, 2 * LANES), BF16)


def half_tile(whole, half, sources, ref, plan):
    return gather_tile(whole, sources, lambda n: ref[n], plan)[:, half]


def backward_starts(plan):
    low, high = HALO - plan.group, HALO + 2 * plan.group
    found = []
    for unused in range(plan.layers):
        found.append(starts(low, high, plan.span) if high - low >= plan.span else [HALO - 2])
        low, high = low + 1, high - 1
    return found


def probabilities(act, matrix, plan):
    logits = jnp.dot(act, matrix, preferred_element_type=F32)
    lane = lax.broadcasted_iota(jnp.int32, (1, LANES), 1)
    probs = []
    for v in range(plan.group):
        exponent = jnp.where(lane < plan.classes, jnp.exp(logits[:, v * LANES : (v + 1) * LANES]), 0.0)
        probs.append(exponent / jnp.sum(exponent, axis=1, keepdims=True))
    return probs


def backward_kernel(plan, weights_ref, head_ref, msg_ref, got_ref, pre4_ref, label_ref, act_ref, pre_ref, out_ref, band, xs, src, grads, dlog):
    ch, span, tile, m, rows = plan.channels, plan.span, plan.tile, plan.m, plan.rows
    group, own = plan.group, plan.own
    base = position(plan) * own - HALO
    peer = lax.axis_index("peer")
    build_bands(weights_ref, band, plan)
    clear_edges(xs, 2, plan)
    own_matrix = head_matrix(head_ref[...], plan)
    matrices = [head_matrix(got_ref[q, m : m + ch, 0:LANES], plan) for q in range(plan.n_peer - 1)]
    lane = lax.broadcasted_iota(jnp.int32, (1, LANES), 1)
    step = min(m, 128)

    for g in range(3):
        cols = slice(g * LANES, (g + 1) * LANES)
        voxel = HALO + (g - 1) * group + lane // ch
        inside = crop_mask(voxel, base, plan)

        def part(c, carry, g=g, cols=cols, inside=inside):
            at = pl.ds(pl.multiple_of(c * step, step), step)
            probs = probabilities(msg_ref[at, cols], own_matrix, plan)
            labels = label_ref[at, :]
            match = labels[:, LANES - plan.slab_depth : LANES - plan.slab_depth + 1]
            shared = [jnp.where(match == peer.astype(F32), x.astype(BF16).astype(F32), 0.0) for x in probs]
            for q in range(plan.n_peer - 1):
                owner = lax.rem(peer - q - 1 + plan.n_peer, plan.n_peer).astype(F32)
                other = probabilities(got_ref[q, at, cols], matrices[q], plan)
                shared = [
                    jnp.where(match == owner, x.astype(BF16).astype(F32), y) for x, y in zip(other, shared)
                ]
            for v in range(group):
                label = labels[:, g * group + v : g * group + v + 1]
                onehot = jnp.where(label == lane.astype(F32), 0.5, 0.0)
                dlog[at, v * LANES : (v + 1) * LANES] = (probs[v] - onehot - 0.5 * shared[v]).astype(BF16)
            back = lax.dot_general(
                dlog[at, :], own_matrix, (((1,), (1,)), ((), ())), preferred_element_type=F32
            )
            value = back * slope(pre4_ref[at, cols])
            src[g, at, 0:LANES] = jnp.where(inside, value, 0.0).astype(BF16).astype(F32)
            return carry

        lax.fori_loop(0, m // step, part, 0)
        if g == 1:
            wide = lax.dot_general(
                msg_ref[0:m, cols], dlog[...], (((0,), (0,)), ((), ())), preferred_element_type=F32
            )
            head_grad = jnp.zeros((ch, LANES), F32)
            for v in range(own):
                head_grad = head_grad + wide[v * ch : (v + 1) * ch, v * LANES : (v + 1) * LANES]
            grads[pl.ds(plan.layers * plan.lane_blocks * ch, ch), :] = head_grad
    if plan.n * plan.chunk > plan.grad_rows:
        grads[plan.grad_rows :, :] = jnp.zeros((plan.n * plan.chunk - plan.grad_rows, LANES), F32)

    wide_lane = lax.broadcasted_iota(jnp.int32, (1, tile), 1)
    begins = backward_starts(plan)
    pre_base = [0] * plan.layers
    for layer in range(1, plan.layers - 1):
        pre_base[layer] = pre_base[layer - 1] + len(begins[plan.layers - 1 - layer])
    sources = None
    mine = lane < own * ch
    for layer in reversed(range(plan.layers)):
        begin = begins[plan.layers - 1 - layer]
        if sources is None:
            before, center, after = src[0, :, 0:LANES], src[1, :, 0:LANES], src[2, :, 0:LANES]
            tiles = [jnp.concatenate([center, before], axis=1), jnp.concatenate([center, after], axis=1)]
        else:
            center = gather_tile(HALO, sources, lambda n: src[n][:, 0:LANES], plan, LANES)
            tiles = [gather_tile(s, sources, lambda n: src[n], plan) for s in begin]
        turned = jnp.where(mine, center, 0.0).T.astype(BF16)
        store_shifted(xs, 2, act_ref[layer].astype(F32), plan)
        blocks = [jnp.zeros((ch, tile), F32) for unused in range(round_up(plan.lane_blocks, 2) // 2)]
        for ij in range(9):
            i, j = divmod(ij, 3)
            product = jnp.dot(turned, xs[2, j, i * rows : i * rows + m, :], preferred_element_type=F32)
            target = ij * 3 * ch
            total = None
            for b in range(own):
                shift = (target - (b - 1) * ch) % tile
                piece = product[b * ch : (b + 1) * ch]
                piece = pltpu.roll(piece, shift, 1) if shift else piece
                total = piece if total is None else total + piece
            for q in range(target // tile, (target + 3 * ch - 1) // tile + 1):
                place = wide_lane + q * tile
                blocks[q] = jnp.where((place >= target) & (place < target + 3 * ch), total, blocks[q])
        for q in range(plan.lane_blocks):
            at = (layer * plan.lane_blocks + q) * ch
            grads[at : at + ch, :] = blocks[q // 2][:, (q % 2) * LANES : (q % 2 + 1) * LANES]
        for t, value in enumerate(tiles):
            store_shifted(xs, t, value, plan)

        def one(t, carry, layer=layer, begin=begin):
            total = None
            for ij in range(9):
                i, j = divmod(ij, 3)
                term = lax.dot_general(
                    xs[t, 2 - j, (2 - i) * rows : (2 - i) * rows + m, :],
                    band[layer, ij * tile : (ij + 1) * tile, :],
                    (((1,), (1,)), ((), ())),
                    preferred_element_type=F32,
                )
                total = term if total is None else total + term
            if layer > 0:
                begin_t = begin[0] if len(begin) == 1 else jnp.where(t == 0, begin[0], begin[1])
                residue = wide_lane // ch
                voxel = begin_t + lax.rem(residue - lax.rem(begin_t, span) + span, span)
                value = total * slope(pre_ref[pre_base[layer - 1] + t])
                src[t] = jnp.where(crop_mask(voxel, base, plan), value, 0.0).astype(BF16).astype(F32)
            else:
                src[t] = total
            return carry

        lax.fori_loop(0, len(begin), one, 0)
        sources = [(s + 1, s + span - 1) for s in begin]
    back = gather_tile(HALO, sources, lambda n: src[n][:, 0:LANES], plan, LANES)
    for d in range(plan.n_depth):
        for r in range(plan.n_row):
            p = d * plan.n_row + r
            parts = [grads[p * plan.chunk : (p + 1) * plan.chunk, :]]
            for k in range(plan.slab_depth):
                at = (d * plan.slab_depth + k) * rows + r * plan.slab_rows
                parts.append(back[at : at + plan.slab_rows])
            spare = plan.back_rows - plan.chunk - plan.slab
            if spare:
                parts.append(jnp.zeros((spare, LANES), F32))
            out_ref[p] = jnp.concatenate(parts, axis=0).astype(BF16)


def slope(pre):
    value = pre.astype(F32)
    sigma = 1.0 / (1.0 + jnp.exp(-value))
    return sigma * (1.0 + value * (1.0 - sigma))


def sum_kernel(plan, recv_ref, out_ref, back_ref):
    total = None
    backs = []
    for p in range(plan.n):
        value = recv_ref[p].astype(F32)
        part = value[0 : plan.chunk]
        total = part if total is None else total + part
        backs.append(value[plan.chunk : plan.chunk + plan.slab])
    total = total.astype(BF16)
    for p in range(plan.n):
        out_ref[p] = total
    lanes = plan.own * plan.channels
    step = LANES // lanes
    for q in range(plan.n // step):
        pieces = [backs[q * step + u][:, 0:lanes] for u in range(step)]
        piece = pieces[0] if step == 1 else jnp.concatenate(pieces, axis=1)
        for k in range(plan.slab_depth):
            rows = piece[k * plan.slab_rows : (k + 1) * plan.slab_rows]
            back_ref[k, :, q * LANES : (q + 1) * LANES] = rows.astype(BF16)


def unpack_kernel(plan, recv_ref, conv_ref, head_ref):
    ch = plan.channels
    rows = [recv_ref[p].astype(F32) for p in range(plan.n)]
    flat = jnp.concatenate(rows, axis=0)
    for layer in range(plan.layers):
        for q in range(plan.lane_blocks):
            at = (layer * plan.lane_blocks + q) * ch
            count = min(LANES, plan.taps - q * LANES)
            turned = flat[at : at + ch].T
            conv_ref[0, layer, q * LANES : q * LANES + count, :] = turned[0:count]
    at = plan.layers * plan.lane_blocks * ch
    head_ref[0] = flat[at : at + ch, 0 : plan.classes]


def call(kernel, plan, out_shape, scratch=(), smem=0, inputs=1):
    vmem = pl.BlockSpec(memory_space=pltpu.VMEM)
    specs = [pl.BlockSpec(memory_space=pltpu.SMEM)] * smem + [vmem] * (inputs - smem)
    many = isinstance(out_shape, (list, tuple))
    return pl.pallas_call(
        functools.partial(kernel, plan),
        out_shape=out_shape,
        in_specs=specs,
        out_specs=[vmem] * len(out_shape) if many else vmem,
        scratch_shapes=list(scratch),
        compiler_params=pltpu.CompilerParams(vmem_limit_bytes=48 * 1024 * 1024),
    )


def body(mesh, features, labels, conv_weights, head_weights, matching):
    plan = Plan(mesh, features, labels, conv_weights, head_weights)
    shape = jax.ShapeDtypeStruct
    m, ch, tile, n = plan.m, plan.channels, plan.tile, plan.n
    head = jnp.pad(head_weights[0], ((0, 0), (0, LANES - plan.classes)))
    chunk_rows = plan.blocks * plan.slab + plan.slab_rows
    packed = call(pack_kernel, plan, shape((n, chunk_rows, LANES), BF16), smem=1, inputs=3)(
        matching, features, labels
    )
    slabs = lax.all_to_all(packed, GROUP, 0, 0, tiled=True)
    n_pre = sum(len(b) for b in backward_starts(plan)[:-1])
    padded = m + 2 * plan.rows
    band = pltpu.VMEM((plan.layers, 9 * tile, tile), BF16)
    message, pre4, label_rows, acts, pres = call(
        forward_kernel,
        plan,
        [
            shape((m + ch, 3 * LANES), BF16),
            shape((m, 3 * LANES), BF16),
            shape((m, LANES), F32),
            shape((plan.layers, m, tile), BF16),
            shape((n_pre, m, tile), BF16),
        ],
        [
            band,
            pltpu.VMEM((3, 3, padded, tile), BF16),
            pltpu.VMEM((3, m, tile), F32),
            pltpu.VMEM((3, m, tile), F32),
        ],
        inputs=3,
    )(slabs, conv_weights, head)
    peers = plan.n_peer
    got = jnp.stack(
        [lax.ppermute(message, "peer", [(i, (i + q) % peers) for i in range(peers)]) for q in range(1, peers)]
    )
    parts = call(
        backward_kernel,
        plan,
        shape((n, plan.back_rows, LANES), BF16),
        [
            band,
            pltpu.VMEM((3, 3, padded, tile), BF16),
            pltpu.VMEM((3, m, tile), F32),
            pltpu.VMEM((n * plan.chunk, LANES), F32),
            pltpu.VMEM((m, plan.group * LANES), BF16),
        ],
        inputs=8,
    )(conv_weights, head, message, got, pre4, label_rows, acts, pres)
    parts = lax.all_to_all(parts, GROUP, 0, 0, tiled=True)
    sums, input_grads = call(
        sum_kernel,
        plan,
        [shape((n, plan.chunk, LANES), BF16), shape(features.shape, BF16)],
    )(parts)
    sums = lax.all_to_all(sums, GROUP, 0, 0, tiled=True)
    conv_grads, head_grads = call(
        unpack_kernel,
        plan,
        [shape((1,) + conv_weights.shape[1:], F32), shape((1, ch, plan.classes), F32)],
    )(sums)
    return conv_grads, head_grads, input_grads[None]


def solution(mesh):
    placed = (
        P("depth", "row", None),
        P("depth", "row", None),
        P("peer", None, None, None),
        P("peer", None, None),
        P("depth", None),
    )
    return jax.shard_map(
        functools.partial(body, mesh),
        mesh=mesh,
        in_specs=placed,
        out_specs=(
            P("peer", None, None, None),
            P("peer", None, None),
            P("peer", "depth", "row", None),
        ),
        check_vma=False,
    )
```

```python
import functools

import jax
import jax.numpy as jnp
from jax import lax
from jax.experimental import pallas as pl
from jax.experimental.pallas import tpu as pltpu
from jax.sharding import PartitionSpec as P

LANES = 128
PAIR = 2 * LANES
F32 = jnp.float32
BF16 = jnp.bfloat16
GROUP = ("depth", "row")


def round_up(value, step):
    return -(-value // step) * step


class Plan:
    def __init__(self, mesh, features, labels, conv_weights, head_weights):
        self.n_depth = mesh.shape["depth"]
        self.n_row = mesh.shape["row"]
        self.n_peer = mesh.shape["peer"]
        self.n = self.n_depth * self.n_row
        self.slab_depth, self.slab_rows, merged = features.shape
        self.layers, self.taps, self.channels = conv_weights.shape[1:]
        self.classes = head_weights.shape[2]
        self.width = merged // self.channels
        self.depth = self.slab_depth * self.n_depth
        self.rows = self.slab_rows * self.n_row
        self.m = self.depth * self.rows
        self.slab = self.slab_depth * self.slab_rows
        self.own = self.width // self.n
        self.group = LANES // self.channels
        self.halo = 2 * self.layers
        self.blocks = round_up(2 * self.halo + self.own, self.group) // self.group
        self.window = self.blocks * self.group
        self.top = self.window - 2 * self.layers
        self.top_blocks = round_up(self.top, self.group) // self.group
        self.lane_blocks = round_up(self.taps, LANES) // LANES
        spare = self.lane_blocks * LANES - self.taps
        self.spare = spare if spare * self.layers >= self.classes else 0
        self.grad_rows = (self.layers * self.lane_blocks + (0 if self.spare else 1)) * self.channels
        self.chunk = round_up(-(-self.grad_rows // self.n), 8)
        self.back_rows = round_up(self.chunk + self.slab, 8)


def crop_mask(block, level, base, plan):
    place = base + block * plan.group + level + lax.broadcasted_iota(jnp.int32, (1, LANES), 1) // plan.channels
    return (place >= 0) & (place < plan.width)


def first_half():
    return lax.broadcasted_iota(jnp.int32, (1, LANES), 1) < LANES // 2


def position(plan):
    return lax.axis_index("depth") * plan.n_row + lax.axis_index("row")


def clear_edges(xs, plan):
    rows = plan.rows
    zero = jnp.zeros((rows, LANES), BF16)
    for slot in range(xs.shape[0]):
        xs[slot, 0:rows, :] = zero
        xs[slot, rows + plan.m : 2 * rows + plan.m, :] = zero


def fill_odd(xs, slots, plan):
    at = slice(plan.rows, plan.rows + plan.m)
    for t in slots:
        xs[t, at, :] = jnp.where(first_half(), xs[t + 1, at, :], xs[t - 1, at, :])


def convolve(xs, slots, matrix, plan):
    m, rows = plan.m, plan.rows
    row = lax.rem(lax.broadcasted_iota(jnp.int32, (m, 1), 0), rows)
    parts = []
    for half, slot in enumerate(slots):
        if slot is None:
            parts.append(None)
            continue
        lhs = jnp.concatenate([xs[slot, i * rows : i * rows + m, :] for i in range(3)], axis=1)
        parts.append(jnp.dot(lhs, matrix(half), preferred_element_type=F32))
    left, right = (parts[0] if parts[0] is not None else parts[1]), (parts[1] if parts[1] is not None else parts[0])
    mask = first_half()
    center = jnp.where(mask, left[:, :LANES], right[:, :LANES])
    before = pltpu.roll(jnp.where(mask, right[:, :LANES], left[:, :LANES]), LANES // 2, 1)
    after = jnp.where(mask, left[:, LANES:], right[:, LANES:])
    before = jnp.where(row == 0, 0.0, pltpu.roll(before, 1, 0))
    after = jnp.where(row == rows - 1, 0.0, pltpu.roll(after, m - 1, 0))
    return before + center + after


SLOTS = ({1: 0, 0: 2, 2: 4}, {0: 0, 1: 2, 2: 6})


def lane_masks(plan):
    place = lax.broadcasted_iota(jnp.int32, (plan.channels, PAIR), 1) // plan.channels
    return [(place == q).astype(BF16) for q in range(PAIR // plan.channels)]


def band_rows(term, forward, i, p, half, masks):
    turned = (half == 1) if forward else (half == 0)
    f = (p - 2) % 4 if turned else p
    total = None
    for o in range(2):
        k = f - o if forward else o + 2 - f
        if not 0 <= k <= 2:
            continue
        for j in range(3):
            ij = 3 * i + j if forward else 3 * (2 - i) + 2 - j
            piece = term(3 * ij + k) * masks[SLOTS[half][j] + o]
            total = piece if total is None else total + piece
    return total


def band_kernel(plan, peers, backward, turned_ref, *refs):
    ch, group = plan.channels, plan.group
    outs, (wide, tall) = refs[:-2], refs[-2:]
    eye_r = lax.broadcasted_iota(jnp.int32, (ch, PAIR), 0)
    eye_l = lax.broadcasted_iota(jnp.int32, (ch, PAIR), 1)
    spread = (eye_r == lax.rem(eye_l, ch)).astype(BF16)
    zero = jnp.zeros_like(spread)
    spreads = jnp.concatenate(
        [jnp.concatenate([spread if u == v else zero for u in range(group)], axis=1) for v in range(group)], axis=0
    )
    masks = lane_masks(plan)
    for peer in range(peers):
        for layer in range(plan.layers):
            weights = turned_ref[peer, layer]
            wide[layer] = lax.dot_general(
                weights, spread, (((0,), (0,)), ((), ())), preferred_element_type=F32
            ).astype(BF16)
            for q in range(plan.lane_blocks if backward else 0):
                count = min(LANES, plan.taps - q * LANES)
                part = jnp.dot(
                    weights[:, q * LANES : q * LANES + count], spreads[0:count], preferred_element_type=F32
                ).astype(BF16)
                for u in range(count // ch):
                    tall[layer, q * group + u] = part[:, u * PAIR : (u + 1) * PAIR]

        def one(layer, carry, peer=peer):
            for half in range(2):
                for i in range(3):
                    for p in range(group):
                        at = slice((i * group + p) * ch, (i * group + p + 1) * ch)
                        outs[0][peer, layer, half, at, :] = band_rows(
                            lambda n: wide[layer, n * ch : (n + 1) * ch, :], True, i, p, half, masks
                        )
                        if backward:
                            outs[1][peer, layer, half, at, :] = band_rows(
                                lambda n: tall[layer, n], False, i, p, half, masks
                            )
            return carry

        lax.fori_loop(0, plan.layers, one, 0)


def head_matrix(head, plan):
    ch, group = plan.channels, plan.group
    lanes = lax.broadcasted_iota(jnp.int32, (ch, group * LANES), 1) // LANES
    wide = jnp.concatenate([head] * group, axis=1)
    zero = jnp.zeros_like(wide)
    return jnp.concatenate([jnp.where(lanes == v, wide, zero) for v in range(group)], axis=0)


def pack_kernel(plan, match_hbm, feat_hbm, label_hbm, out_ref, match_ref, feat_ref, label_ref, sems):
    ch, own = plan.channels, plan.own
    copies = [
        pltpu.make_async_copy(source, target, sems.at[n])
        for n, (source, target) in enumerate(((feat_hbm, feat_ref), (label_hbm, label_ref), (match_hbm, match_ref)))
    ]
    for copy in copies:
        copy.start()
    for copy in copies:
        copy.wait()
    feats = feat_ref[...].astype(F32).reshape(plan.slab, plan.width * ch)
    labels = label_ref[...].astype(F32)
    peer = lax.axis_index("peer")
    lane = lax.broadcasted_iota(jnp.int32, (plan.slab_rows, LANES), 1)
    seen = 3 * plan.group
    matches = jnp.zeros((plan.slab_rows, LANES), F32)
    for k in range(plan.slab_depth):
        matches = jnp.where(lane == LANES - plan.slab_depth + k, match_ref[peer, k].astype(F32), matches)

    def cut(array, low, high, limit):
        pieces = []
        if low < 0:
            pieces.append(jnp.zeros((array.shape[0], min(-low, high - low)), F32))
        if max(low, 0) < min(high, limit):
            pieces.append(array[:, max(low, 0) : min(high, limit)])
        if high > limit:
            pieces.append(jnp.zeros((array.shape[0], min(high - limit, high - low)), F32))
        return jnp.concatenate(pieces, axis=1) if len(pieces) > 1 else pieces[0]

    for p in range(plan.n):
        first = p * own - plan.halo
        parts = []
        for q in range(plan.blocks):
            low = (first + q * plan.group) * ch
            parts.append(cut(feats, low, low + LANES, plan.width * ch))
        low = p * own + plan.layers - plan.halo
        pieces = []
        for k in range(plan.slab_depth):
            pieces.append(cut(labels[k], low, low + seen, plan.width))
        pieces.append(jnp.zeros((plan.slab_rows, LANES - plan.slab_depth * seen), F32))
        parts.append(jnp.concatenate(pieces, axis=1) + matches)
        out_ref[p] = jnp.concatenate(parts, axis=0).astype(BF16)


def unpack_slabs(plan, recv_ref, source, label_ref):
    rows = plan.rows
    lane = lax.broadcasted_iota(jnp.int32, (1, LANES), 1)
    seen = 3 * plan.group
    keep = LANES - plan.slab_depth
    for d in range(plan.n_depth):
        parts = [recv_ref[d * plan.n_row + r].astype(F32) for r in range(plan.n_row)]
        for k in range(plan.slab_depth):
            at = (d * plan.slab_depth + k) * rows
            for q in range(plan.blocks + 1):
                low = q * plan.slab + k * plan.slab_rows if q < plan.blocks else plan.blocks * plan.slab
                piece = jnp.concatenate([x[low : low + plan.slab_rows] for x in parts], axis=0)
                if q < plan.blocks:
                    source[2 * q, rows + at : rows + at + rows, :] = piece.astype(BF16)
                    continue
                if k > 0:
                    moved = pltpu.roll(piece, LANES - k * seen, 1)
                    piece = jnp.where(lane < seen, moved, pltpu.roll(piece, LANES - k, 1))
                label_ref[at : at + rows, :] = jnp.where((lane < seen) | (lane == keep), piece, 0.0)


def forward(plan, buffers, first, matrix, base, keep):
    m, rows, group = plan.m, plan.rows, plan.group
    at = slice(rows, rows + m)
    count = plan.window
    source = buffers[first]
    for layer in range(plan.layers):
        target = buffers[1 + layer % 2]
        fill_odd(source, range(1, (count - 4) // 2 + 1, 2), plan)
        keep(layer, source)
        count -= 2
        for b in range(round_up(count, group) // group):
            slots = (2 * b, 2 * b + 1 if b * group + 2 < count else None)
            total = convolve(source, slots, lambda half: matrix(layer, half), plan)
            keep(layer, None, b, total)
            value = total / (1.0 + jnp.exp(-total))
            target[2 * b, at, :] = jnp.where(crop_mask(b, layer + 1, base, plan), value, 0.0).astype(BF16)
        source = target
    return source


def class_ones(plan):
    rows = lax.broadcasted_iota(jnp.int32, (2 * LANES, 2 * LANES), 0)
    lanes = lax.broadcasted_iota(jnp.int32, (2 * LANES, 2 * LANES), 1)
    return (rows // LANES == lanes // LANES).astype(BF16)


def probabilities(act, matrix, ones, plan):
    logits = jnp.dot(act, matrix, preferred_element_type=F32)
    lane = lax.rem(lax.broadcasted_iota(jnp.int32, (1, 2 * LANES), 1), LANES)
    probs = []
    for v in range(0, plan.group, 2):
        exponent = jnp.where(lane < plan.classes, jnp.exp(logits[:, v * LANES : (v + 2) * LANES]), 0.0)
        high = exponent.astype(BF16)
        rest = (exponent - high.astype(F32)).astype(BF16)
        total = jnp.dot(high, ones, preferred_element_type=F32) + jnp.dot(rest, ones, preferred_element_type=F32)
        probs.append(exponent / total)
    return probs


def main_kernel(plan, recv_ref, band_hbm, back_hbm, other_hbm, head_ref, heads_ref, out_ref, *scratch):
    slabs, one_xs, two_xs, acts, pres, label_ref, part, dlog, grads, band, back_band, other_band, sems = scratch
    ch, m, rows, group, own, layers = plan.channels, plan.m, plan.rows, plan.group, plan.own, plan.layers
    base = position(plan) * own - plan.halo
    peer = lax.axis_index("peer")
    copies = [pltpu.make_async_copy(band_hbm.at[0, n], band.at[n], sems.at[n]) for n in range(layers)]
    copies.append(pltpu.make_async_copy(back_hbm.at[0], back_band, sems.at[layers]))
    first = pltpu.make_async_copy(other_hbm.at[0], other_band, sems.at[layers + 1])
    for copy in copies:
        copy.start()
    first.start()
    buffers = (slabs, one_xs, two_xs)
    for xs in buffers:
        clear_edges(xs, plan)
    unpack_slabs(plan, recv_ref, slabs, label_ref)
    at = slice(rows, rows + m)
    lane = lax.broadcasted_iota(jnp.int32, (1, LANES), 1)
    half_mask = first_half()

    def keep(layer, source, b=None, total=None):
        if source is not None:
            copies[layer].wait()
            if layer == 0:
                acts[0, :, 0:LANES] = jnp.where(half_mask, source[6, at, :], source[2, at, :])
            else:
                acts[layer, :, 0:LANES] = source[2, at, :]
            acts[layer, :, LANES:PAIR] = source[4, at, :]
        elif b < plan.top_blocks:
            pres[layer, b] = total.astype(BF16)

    last = forward(plan, buffers, 0, lambda layer, half: band[layer, half], base, keep)
    own_matrix = head_matrix(head_ref[...], plan)
    ones = class_ones(plan)
    pair_lane = lax.rem(lax.broadcasted_iota(jnp.int32, (1, PAIR), 1), LANES).astype(F32)
    spread_r = lax.broadcasted_iota(jnp.int32, (LANES, PAIR), 0)
    spread_l = lax.broadcasted_iota(jnp.int32, (LANES, PAIR), 1) // LANES
    labels = label_ref[...]
    codes = labels.astype(BF16)
    match = labels[:, LANES - plan.slab_depth : LANES - plan.slab_depth + 1]
    weight = jnp.where(match == peer.astype(F32), 0.5, 0.0)
    for g in range(3):
        for u, value in enumerate(probabilities(last[2 * g, at, :], own_matrix, ones, plan)):
            place = g * group + 2 * u
            spread = (spread_r == spread_l + place).astype(BF16)
            label = jnp.dot(codes, spread, preferred_element_type=F32)
            onehot = jnp.where(label == pair_lane, 0.5, 0.0)
            part[:, place * LANES : place * LANES + PAIR] = (
                value - onehot - weight * value.astype(BF16).astype(F32)
            )
    hidden = last[2, at, :]

    def other(q, carry):
        if plan.n_peer > 2:

            @pl.when(q > 0)
            def fetch():
                copy = pltpu.make_async_copy(other_hbm.at[q], other_band, sems.at[layers + 2])
                copy.start()
                copy.wait()

        owner = lax.rem(peer - q - 1 + plan.n_peer, plan.n_peer)
        last = forward(plan, buffers, 0, lambda layer, half: other_band[layer, half], base, lambda *unused: None)
        matrix = head_matrix(heads_ref[q], plan)
        weight = jnp.where(match == owner.astype(F32), 0.5, 0.0)
        for g in range(3):
            for u, value in enumerate(probabilities(last[2 * g, at, :], matrix, ones, plan)):
                cols = slice((g * group + 2 * u) * LANES, (g * group + 2 * u + 2) * LANES)
                part[:, cols] = part[:, cols] - weight * value.astype(BF16).astype(F32)
        return carry

    first.wait()
    if plan.n_peer == 2:
        other(0, 0)
    else:
        lax.fori_loop(0, plan.n_peer - 1, other, 0)

    wide = group * LANES
    dlog[...] = part[...].astype(BF16)
    level = one_xs
    for g in range(3):
        back = lax.dot_general(
            dlog[:, g * wide : (g + 1) * wide], own_matrix, (((1,), (1,)), ((), ())), preferred_element_type=F32
        )
        value = jnp.where(crop_mask(g, layers, base, plan), back * slope(pres[layers - 1, g]), 0.0)
        level[2 * g, at, :] = value.astype(BF16)
    product = lax.dot_general(
        hidden, dlog[:, wide : 2 * wide], (((0,), (0,)), ((), ())), preferred_element_type=F32
    )
    head_grad = jnp.zeros((ch, LANES), F32)
    for v in range(own):
        head_grad = head_grad + product[v * ch : (v + 1) * ch, v * LANES : (v + 1) * LANES]
    if not plan.spare:
        low = layers * plan.lane_blocks * ch
        grads[low : low + ch, :] = head_grad
    if plan.n * plan.chunk > plan.grad_rows:
        grads[plan.grad_rows :, :] = jnp.zeros((plan.n * plan.chunk - plan.grad_rows, LANES), F32)

    row = lax.rem(lax.broadcasted_iota(jnp.int32, (m, 1), 0), rows)
    wide_lane = lax.broadcasted_iota(jnp.int32, (1, PAIR), 1)
    copies[layers].wait()
    for layer in reversed(range(layers)):
        u = plan.halo - layer - 1
        place = lax.rem(lane // ch - u % group + group, group)
        center = level[2 * (u // group), at, :].astype(F32)
        if u % group:
            center = jnp.where(lane // ch >= u % group, center, level[2 * (u // group) + 2, at, :].astype(F32))
        if own < group:
            center = jnp.where(place < own, center, 0.0)
        shifted = [
            jnp.where(row == rows - 1, 0.0, pltpu.roll(center, m - 1, 0)),
            center,
            jnp.where(row == 0, 0.0, pltpu.roll(center, 1, 0)),
        ]
        turned = jnp.concatenate([x.T.astype(BF16) for x in shifted], axis=0)
        slabs[0, at, :] = acts[layer, :, 0:LANES]
        slabs[1, at, :] = acts[layer, :, LANES:PAIR]
        blocks = [jnp.zeros((ch, PAIR), F32) for unused in range(round_up(plan.lane_blocks, 2) // 2)]
        for i in range(3):
            rhs = jnp.concatenate([slabs[n, i * rows : i * rows + m, :] for n in range(2)], axis=1)
            product = jnp.dot(turned, rhs, preferred_element_type=F32)
            for j in range(3):
                target = (3 * i + j) * 3 * ch
                total = None
                for b in range(own):
                    shift = (target - ((plan.halo + b - 1 - layer - group) % (2 * group)) * ch) % PAIR
                    low = j * LANES + ((u + b) % group) * ch
                    piece = product[low : low + ch]
                    piece = pltpu.roll(piece, shift, 1) if shift else piece
                    total = piece if total is None else total + piece
                for q in range(target // PAIR, (target + 3 * ch - 1) // PAIR + 1):
                    spot = wide_lane + q * PAIR
                    blocks[q] = jnp.where((spot >= target) & (spot < target + 3 * ch), total, blocks[q])
        for q in range(plan.lane_blocks):
            low = (layer * plan.lane_blocks + q) * ch
            block = blocks[q // 2][:, (q % 2) * LANES : (q % 2 + 1) * LANES]
            if plan.spare and q == plan.lane_blocks - 1:
                moved = pltpu.roll(head_grad, (LANES - plan.spare - layer * plan.spare) % LANES, 1)
                block = jnp.where(lane < LANES - plan.spare, block, moved)
            grads[low : low + ch, :] = block
        start = 2 * (layers - layer)
        target = two_xs if level is one_xs else one_xs
        fill_odd(level, [t for t in range(start // 2 - 1, plan.top // 2 - 1) if t % 2], plan)
        for b in range(start // group, plan.top_blocks):
            slots = (2 * b - 1 if b * group >= start else None, 2 * b)
            total = convolve(level, slots, lambda half: back_band[layer, half], plan)
            if layer > 0:
                total = total * slope(pres[layer - 1, b])
                target[2 * b, at, :] = jnp.where(crop_mask(b, layer, base, plan), total, 0.0).astype(BF16)
            else:
                result = total
        level = target

    for d in range(plan.n_depth):
        for r in range(plan.n_row):
            p = d * plan.n_row + r
            parts = [grads[p * plan.chunk : (p + 1) * plan.chunk, :]]
            for k in range(plan.slab_depth):
                low = (d * plan.slab_depth + k) * rows + r * plan.slab_rows
                parts.append(result[low : low + plan.slab_rows])
            spare = plan.back_rows - plan.chunk - plan.slab
            if spare:
                parts.append(jnp.zeros((spare, LANES), F32))
            out_ref[p] = jnp.concatenate(parts, axis=0).astype(BF16)


def slope(pre):
    value = pre.astype(F32)
    sigma = 1.0 / (1.0 + jnp.exp(-value))
    return sigma * (1.0 + value * (1.0 - sigma))


def sum_kernel(plan, recv_ref, out_ref, back_ref):
    total = None
    backs = []
    for p in range(plan.n):
        value = recv_ref[p].astype(F32)
        part = value[0 : plan.chunk]
        total = part if total is None else total + part
        backs.append(value[plan.chunk : plan.chunk + plan.slab])
    total = total.astype(BF16)
    for p in range(plan.n):
        out_ref[p] = total
    lanes = plan.own * plan.channels
    step = LANES // lanes
    for q in range(plan.n // step):
        pieces = [backs[q * step + u][:, 0:lanes] for u in range(step)]
        piece = pieces[0] if step == 1 else jnp.concatenate(pieces, axis=1)
        for k in range(plan.slab_depth):
            rows = piece[k * plan.slab_rows : (k + 1) * plan.slab_rows]
            back_ref[k, :, q * LANES : (q + 1) * LANES] = rows.astype(BF16)


def unpack_kernel(plan, recv_ref, conv_ref, head_ref):
    ch = plan.channels
    flat = jnp.concatenate([recv_ref[p].astype(F32) for p in range(plan.n)], axis=0)
    lane = lax.broadcasted_iota(jnp.int32, (1, LANES), 1)
    head = flat[plan.layers * plan.lane_blocks * ch :][0:ch] if not plan.spare else jnp.zeros((ch, LANES), F32)
    for layer in range(plan.layers):
        for q in range(plan.lane_blocks):
            at = (layer * plan.lane_blocks + q) * ch
            count = min(LANES, plan.taps - q * LANES)
            block = flat[at : at + ch]
            conv_ref[0, layer, :, q * LANES : q * LANES + count] = block[:, 0:count]
            if plan.spare and q == plan.lane_blocks - 1:
                moved = pltpu.roll(block, (plan.spare + layer * plan.spare) % LANES, 1)
                head = jnp.where((lane >= layer * plan.spare) & (lane < (layer + 1) * plan.spare), moved, head)
    head_ref[0] = head[:, 0 : plan.classes]


def hbm(array):
    return pltpu.with_memory_space_constraint(array, pltpu.HBM)


def call(kernel, plan, out_shape, scratch=(), specs=(True,), cost=None, limit=16):
    vmem = pl.BlockSpec(memory_space=pltpu.VMEM)
    anywhere = pl.BlockSpec(memory_space=pl.ANY)
    many = isinstance(out_shape, (list, tuple))
    return pl.pallas_call(
        functools.partial(kernel, plan),
        out_shape=out_shape,
        in_specs=[vmem if x else anywhere for x in specs],
        out_specs=[vmem] * len(out_shape) if many else vmem,
        scratch_shapes=list(scratch),
        compiler_params=pltpu.CompilerParams(vmem_limit_bytes=limit * 1024 * 1024),
        cost_estimate=cost,
    )


def make_bands(plan, turned, backward):
    peers = turned.shape[0]
    shape = jax.ShapeDtypeStruct((peers, plan.layers, 2, 3 * LANES, PAIR), BF16)
    made = call(
        lambda plan, *refs: band_kernel(plan, peers, backward, *refs),
        plan,
        [shape] * (2 if backward else 1),
        [
            pltpu.VMEM((plan.layers, plan.taps, PAIR), BF16),
            pltpu.VMEM((plan.layers, plan.taps // plan.channels, plan.channels, PAIR), BF16),
        ],
        cost=pl.CostEstimate(flops=10**9, bytes_accessed=4 * 10**6, transcendentals=0),
    )(turned)
    return [hbm(x) for x in made]


def from_others(array, peers):
    moved = [lax.ppermute(array, "peer", [(i, (i + q) % peers) for i in range(peers)]) for q in range(1, peers)]
    return moved[0] if len(moved) == 1 else jnp.concatenate(moved, axis=0)


def body(mesh, features, labels, conv_weights, head_weights, matching):
    plan = Plan(mesh, features, labels, conv_weights, head_weights)
    shape = jax.ShapeDtypeStruct
    m, ch, n, layers = plan.m, plan.channels, plan.n, plan.layers
    head = jnp.pad(head_weights, ((0, 0), (0, 0), (0, LANES - plan.classes)))
    chunk_rows = plan.blocks * plan.slab + plan.slab_rows
    packed = call(
        pack_kernel,
        plan,
        shape((n, chunk_rows, LANES), BF16),
        [
            pltpu.SMEM(matching.shape[::-1], jnp.int32),
            pltpu.VMEM(features.shape, BF16),
            pltpu.VMEM(labels.shape, jnp.int32),
            pltpu.SemaphoreType.DMA((3,)),
        ],
        specs=(False,) * 3,
    )(hbm(matching.T), hbm(features), hbm(labels))
    slabs = lax.all_to_all(packed, GROUP, 0, 0, tiled=True)
    turned = jnp.swapaxes(conv_weights, 2, 3)
    others = from_others(turned, plan.n_peer)
    heads = from_others(head, plan.n_peer)
    band, back_band = make_bands(plan, turned, True)
    (other_band,) = make_bands(plan, others, False)
    padded = m + 2 * plan.rows
    wide = 3 * plan.group * LANES
    windows = 2 * plan.blocks
    banded = pltpu.VMEM((layers, 2, 3 * LANES, PAIR), BF16)
    parts = call(
        main_kernel,
        plan,
        shape((n, plan.back_rows, LANES), BF16),
        [
            pltpu.VMEM((windows, padded, LANES), BF16),
            pltpu.VMEM((windows, padded, LANES), BF16),
            pltpu.VMEM((windows, padded, LANES), BF16),
            pltpu.VMEM((layers, m, PAIR), BF16),
            pltpu.VMEM((layers, plan.top_blocks, m, LANES), BF16),
            pltpu.VMEM((m, LANES), F32),
            pltpu.VMEM((m, wide), F32),
            pltpu.VMEM((m, wide), BF16),
            pltpu.VMEM((n * plan.chunk, LANES), F32),
            banded,
            banded,
            banded,
            pltpu.SemaphoreType.DMA((layers + 3,)),
        ],
        specs=(True, False, False, False, True, True),
        limit=48,
    )(slabs, band, back_band, other_band, head[0], heads)
    parts = lax.all_to_all(parts, GROUP, 0, 0, tiled=True)
    sums, input_grads = call(
        sum_kernel,
        plan,
        [shape((n, plan.chunk, LANES), BF16), shape(features.shape, BF16)],
    )(parts)
    sums = lax.all_to_all(sums, GROUP, 0, 0, tiled=True)
    conv_grads, head_grads = call(
        unpack_kernel,
        plan,
        [shape((1, layers, ch, plan.taps), F32), shape((1, ch, plan.classes), F32)],
    )(sums)
    return jnp.swapaxes(conv_grads, 2, 3), head_grads, input_grads[None]


def solution(mesh):
    placed = (
        P("depth", "row", None),
        P("depth", "row", None),
        P("peer", None, None, None),
        P("peer", None, None),
        P("depth", None),
    )
    return jax.shard_map(
        functools.partial(body, mesh),
        mesh=mesh,
        in_specs=placed,
        out_specs=(
            P("peer", None, None, None),
            P("peer", None, None),
            P("peer", "depth", "row", None),
        ),
        check_vma=False,
    )
```

```python
import functools

import jax
import jax.numpy as jnp
from jax import lax
from jax.experimental import pallas as pl
from jax.experimental.pallas import tpu as pltpu
from jax.sharding import PartitionSpec as P

LANES = 128
PAIR = 2 * LANES
F32 = jnp.float32
BF16 = jnp.bfloat16
GROUP = ("depth", "row")
MAIN_MIB = 40
CHUNKS = 3


def round_up(value, step):
    return -(-value // step) * step


class Plan:
    def __init__(self, mesh, features, labels, conv_weights, head_weights):
        self.n_depth = mesh.shape["depth"]
        self.n_row = mesh.shape["row"]
        self.n_peer = mesh.shape["peer"]
        self.n = self.n_depth * self.n_row
        self.slab_depth, self.slab_rows, merged = features.shape
        self.layers, self.taps, self.channels = conv_weights.shape[1:]
        self.classes = head_weights.shape[2]
        self.width = merged // self.channels
        self.depth = self.slab_depth * self.n_depth
        self.rows = self.slab_rows * self.n_row
        self.m = self.depth * self.rows
        self.slab = self.slab_depth * self.slab_rows
        self.own = self.width // self.n
        self.group = LANES // self.channels
        self.halo = 2 * self.layers
        self.blocks = round_up(2 * self.halo + self.own, self.group) // self.group
        self.window = self.blocks * self.group
        self.top = self.window - 2 * self.layers
        self.top_blocks = round_up(self.top, self.group) // self.group
        self.lane_blocks = round_up(self.taps, LANES) // LANES
        spare = self.lane_blocks * LANES - self.taps
        self.spare = spare if spare * self.layers >= self.classes else 0
        self.grad_rows = (self.layers * self.lane_blocks + (0 if self.spare else 1)) * self.channels
        self.chunk = round_up(-(-self.grad_rows // self.n), 8)
        self.back_rows = round_up(self.chunk + self.slab, 8)


def crop_mask(block, level, base, plan):
    place = base + block * plan.group + level + lax.broadcasted_iota(jnp.int32, (1, LANES), 1) // plan.channels
    return (place >= 0) & (place < plan.width)


def first_half():
    return lax.broadcasted_iota(jnp.int32, (1, LANES), 1) < LANES // 2


def position(plan):
    return lax.axis_index("depth") * plan.n_row + lax.axis_index("row")


def clear_edges(xs, plan):
    rows = plan.rows
    zero = jnp.zeros((rows, LANES), BF16)
    for slot in range(xs.shape[0]):
        xs[slot, 0:rows, :] = zero
        xs[slot, rows + plan.m : 2 * rows + plan.m, :] = zero


def fill_odd(xs, slots, plan):
    at = slice(plan.rows, plan.rows + plan.m)
    for t in slots:
        xs[t, at, :] = jnp.where(first_half(), xs[t + 1, at, :], xs[t - 1, at, :])


def convolve(xs, slots, matrix, plan, use):
    rows = plan.rows
    mask = first_half()
    step = plan.m // CHUNKS
    row = lax.rem(lax.broadcasted_iota(jnp.int32, (step, 1), 0), rows)
    for c in range(CHUNKS):
        parts = []
        for half, slot in enumerate(slots):
            if slot is None:
                parts.append(None)
                continue
            low = c * step
            lhs = jnp.concatenate([xs[slot, i * rows + low : i * rows + low + step, :] for i in range(3)], axis=1)
            rhs = jnp.concatenate([matrix(half), matrix(2)], axis=1)
            parts.append(jnp.dot(lhs, rhs, preferred_element_type=F32))
        left = parts[0] if parts[0] is not None else parts[1]
        right = parts[1] if parts[1] is not None else parts[0]
        center = jnp.where(mask, left[:, :LANES], right[:, :LANES])
        before = pltpu.roll(jnp.where(mask, right[:, :LANES], left[:, :LANES]), LANES // 2, 1)
        after = jnp.where(mask, left[:, LANES:], right[:, LANES:])
        before = jnp.where(row == 0, 0.0, pltpu.roll(before, 1, 0))
        after = jnp.where(row == rows - 1, 0.0, pltpu.roll(after, step - 1, 0))
        use(before + center + after, slice(c * step, c * step + step))


SLOTS = ({1: 0, 0: 2, 2: 4}, {0: 0, 1: 2, 2: 6})


def lane_masks(plan):
    place = lax.broadcasted_iota(jnp.int32, (plan.channels, PAIR), 1) // plan.channels
    return [(place == q).astype(BF16) for q in range(PAIR // plan.channels)]


def band_rows(term, forward, i, p, half, masks):
    turned = (half == 1) if forward else (half == 0)
    f = (p - 2) % 4 if turned else p
    total = None
    for o in range(2):
        k = f - o if forward else o + 2 - f
        if not 0 <= k <= 2:
            continue
        for j in range(3):
            ij = 3 * i + j if forward else 3 * (2 - i) + 2 - j
            piece = term(3 * ij + k) * masks[SLOTS[half][j] + o]
            total = piece if total is None else total + piece
    return total


def band_kernel(plan, peers, backward, turned_ref, *refs):
    ch, group = plan.channels, plan.group
    outs, (wide, tall) = refs[:-2], refs[-2:]
    eye_r = lax.broadcasted_iota(jnp.int32, (ch, PAIR), 0)
    eye_l = lax.broadcasted_iota(jnp.int32, (ch, PAIR), 1)
    spread = (eye_r == lax.rem(eye_l, ch)).astype(BF16)
    zero = jnp.zeros_like(spread)
    spreads = jnp.concatenate(
        [jnp.concatenate([spread if u == v else zero for u in range(group)], axis=1) for v in range(group)], axis=0
    )
    masks = lane_masks(plan)
    for peer in range(peers):
        for layer in range(plan.layers):
            weights = turned_ref[peer, layer]
            wide[layer] = lax.dot_general(
                weights, spread, (((0,), (0,)), ((), ())), preferred_element_type=F32
            ).astype(BF16)
            for q in range(plan.lane_blocks if backward else 0):
                count = min(LANES, plan.taps - q * LANES)
                part = jnp.dot(
                    weights[:, q * LANES : q * LANES + count], spreads[0:count], preferred_element_type=F32
                ).astype(BF16)
                for u in range(count // ch):
                    tall[layer, q * group + u] = part[:, u * PAIR : (u + 1) * PAIR]

        def one(layer, carry, peer=peer):
            for out, ahead, term in (
                (outs[0], True, lambda n: wide[layer, n * ch : (n + 1) * ch, :]),
                (outs[-1], False, lambda n: tall[layer, n]),
            )[: len(outs)]:
                for i in range(3):
                    for p in range(group):
                        at = slice((i * group + p) * ch, (i * group + p + 1) * ch)
                        first, second = [band_rows(term, ahead, i, p, half, masks) for half in range(2)]
                        out[peer, layer, 0, at, :] = first[:, :LANES]
                        out[peer, layer, 1, at, :] = second[:, :LANES]
                        out[peer, layer, 2, at, :] = first[:, LANES:] + second[:, LANES:]
            return carry

        lax.fori_loop(0, plan.layers, one, 0)


def head_matrix(head, plan):
    ch, group = plan.channels, plan.group
    lanes = lax.broadcasted_iota(jnp.int32, (ch, group * LANES), 1) // LANES
    wide = jnp.concatenate([head] * group, axis=1)
    zero = jnp.zeros_like(wide)
    return jnp.concatenate([jnp.where(lanes == v, wide, zero) for v in range(group)], axis=0)


def pack_kernel(plan, match_hbm, feat_hbm, label_hbm, out_ref, match_ref, feat_ref, label_ref, sems):
    ch, own = plan.channels, plan.own
    copies = [
        pltpu.make_async_copy(source, target, sems.at[n])
        for n, (source, target) in enumerate(((feat_hbm, feat_ref), (label_hbm, label_ref), (match_hbm, match_ref)))
    ]
    for copy in copies:
        copy.start()
    for copy in copies:
        copy.wait()
    feats = feat_ref[...].astype(F32).reshape(plan.slab, plan.width * ch)
    labels = label_ref[...].astype(F32)
    peer = lax.axis_index("peer")
    lane = lax.broadcasted_iota(jnp.int32, (plan.slab_rows, LANES), 1)
    seen = 3 * plan.group
    matches = jnp.zeros((plan.slab_rows, LANES), F32)
    for k in range(plan.slab_depth):
        matches = jnp.where(lane == LANES - plan.slab_depth + k, match_ref[peer, k].astype(F32), matches)

    def cut(array, low, high, limit):
        pieces = []
        if low < 0:
            pieces.append(jnp.zeros((array.shape[0], min(-low, high - low)), F32))
        if max(low, 0) < min(high, limit):
            pieces.append(array[:, max(low, 0) : min(high, limit)])
        if high > limit:
            pieces.append(jnp.zeros((array.shape[0], min(high - limit, high - low)), F32))
        return jnp.concatenate(pieces, axis=1) if len(pieces) > 1 else pieces[0]

    for p in range(plan.n):
        first = p * own - plan.halo
        parts = []
        for q in range(plan.blocks):
            low = (first + q * plan.group) * ch
            parts.append(cut(feats, low, low + LANES, plan.width * ch))
        low = p * own + plan.layers - plan.halo
        pieces = []
        for k in range(plan.slab_depth):
            pieces.append(cut(labels[k], low, low + seen, plan.width))
        pieces.append(jnp.zeros((plan.slab_rows, LANES - plan.slab_depth * seen), F32))
        parts.append(jnp.concatenate(pieces, axis=1) + matches)
        out_ref[p] = jnp.concatenate(parts, axis=0).astype(BF16)


def unpack_slabs(plan, recv_ref, source, label_ref):
    rows = plan.rows
    lane = lax.broadcasted_iota(jnp.int32, (1, LANES), 1)
    seen = 3 * plan.group
    keep = LANES - plan.slab_depth
    for d in range(plan.n_depth):
        parts = [recv_ref[d * plan.n_row + r].astype(F32) for r in range(plan.n_row)]
        for k in range(plan.slab_depth):
            at = (d * plan.slab_depth + k) * rows
            for q in range(plan.blocks + 1):
                low = q * plan.slab + k * plan.slab_rows if q < plan.blocks else plan.blocks * plan.slab
                piece = jnp.concatenate([x[low : low + plan.slab_rows] for x in parts], axis=0)
                if q < plan.blocks:
                    source[2 * q, rows + at : rows + at + rows, :] = piece.astype(BF16)
                    continue
                if k > 0:
                    moved = pltpu.roll(piece, LANES - k * seen, 1)
                    piece = jnp.where(lane < seen, moved, pltpu.roll(piece, LANES - k, 1))
                label_ref[at : at + rows, :] = jnp.where((lane < seen) | (lane == keep), piece, 0.0)


def forward(plan, buffers, first, matrix, base, keep):
    m, rows, group = plan.m, plan.rows, plan.group
    at = slice(rows, rows + m)
    count = plan.window
    source = buffers[first]
    for layer in range(plan.layers):
        target = buffers[1 + layer % 2]
        fill_odd(source, range(1, (count - 4) // 2 + 1, 2), plan)
        keep(layer, source)
        count -= 2
        for b in range(round_up(count, group) // group):
            slots = (2 * b, 2 * b + 1 if b * group + 2 < count else None)
            inside = crop_mask(b, layer + 1, base, plan)

            def use(total, part, layer=layer, b=b, inside=inside, target=target):
                keep(layer, None, b, total, part)
                value = total / (1.0 + jnp.exp(-total))
                target[2 * b, rows + part.start : rows + part.stop, :] = jnp.where(inside, value, 0.0).astype(BF16)

            convolve(source, slots, lambda half: matrix(layer, half), plan, use)
        source = target
    return source


def class_ones(plan):
    rows = lax.broadcasted_iota(jnp.int32, (2 * LANES, 2 * LANES), 0)
    lanes = lax.broadcasted_iota(jnp.int32, (2 * LANES, 2 * LANES), 1)
    return (rows // LANES == lanes // LANES).astype(BF16)


def probabilities(act, matrix, ones, plan):
    logits = jnp.dot(act, matrix, preferred_element_type=F32)
    lane = lax.rem(lax.broadcasted_iota(jnp.int32, (1, 2 * LANES), 1), LANES)
    probs = []
    for v in range(0, plan.group, 2):
        exponent = jnp.where(lane < plan.classes, jnp.exp(logits[:, v * LANES : (v + 2) * LANES]), 0.0)
        high = exponent.astype(BF16)
        rest = (exponent - high.astype(F32)).astype(BF16)
        total = jnp.dot(high, ones, preferred_element_type=F32) + jnp.dot(rest, ones, preferred_element_type=F32)
        probs.append(exponent / total)
    return probs


def main_kernel(plan, recv_ref, band, back_band, other_band, head_ref, heads_ref, out_ref, *scratch):
    slabs, one_xs, two_xs, acts, pres, label_ref, part, dlog, grads, result = scratch
    ch, m, rows, group, own, layers = plan.channels, plan.m, plan.rows, plan.group, plan.own, plan.layers
    base = position(plan) * own - plan.halo
    peer = lax.axis_index("peer")
    buffers = (slabs, one_xs, two_xs)
    for xs in buffers:
        clear_edges(xs, plan)
    unpack_slabs(plan, recv_ref, slabs, label_ref)
    at = slice(rows, rows + m)
    lane = lax.broadcasted_iota(jnp.int32, (1, LANES), 1)
    half_mask = first_half()

    def keep(layer, source, b=None, total=None, part=None):
        if source is not None:
            if layer == 0:
                acts[0, :, 0:LANES] = jnp.where(half_mask, source[6, at, :], source[2, at, :])
            else:
                acts[layer, :, 0:LANES] = source[2, at, :]
            acts[layer, :, LANES:PAIR] = source[4, at, :]
        elif b < plan.top_blocks:
            pres[layer, b, part, :] = total.astype(BF16)

    last = forward(plan, buffers, 0, lambda layer, half: band[0, layer, half], base, keep)
    own_matrix = head_matrix(head_ref[...], plan)
    ones = class_ones(plan)
    pair_lane = lax.rem(lax.broadcasted_iota(jnp.int32, (1, PAIR), 1), LANES).astype(F32)
    spread_r = lax.broadcasted_iota(jnp.int32, (LANES, PAIR), 0)
    spread_l = lax.broadcasted_iota(jnp.int32, (LANES, PAIR), 1) // LANES
    labels = label_ref[...]
    codes = labels.astype(BF16)
    match = labels[:, LANES - plan.slab_depth : LANES - plan.slab_depth + 1]
    weight = jnp.where(match == peer.astype(F32), 0.5, 0.0)
    for g in range(3):
        for u, value in enumerate(probabilities(last[2 * g, at, :], own_matrix, ones, plan)):
            place = g * group + 2 * u
            spread = (spread_r == spread_l + place).astype(BF16)
            label = jnp.dot(codes, spread, preferred_element_type=F32)
            onehot = jnp.where(label == pair_lane, 0.5, 0.0)
            part[:, place * LANES : place * LANES + PAIR] = (
                value - onehot - weight * value.astype(BF16).astype(F32)
            )
    hidden = last[2, at, :]

    def other(q, carry):
        owner = lax.rem(peer - q - 1 + plan.n_peer, plan.n_peer)
        last = forward(plan, buffers, 0, lambda layer, half: other_band[q, layer, half], base, lambda *unused: None)
        matrix = head_matrix(heads_ref[q], plan)
        weight = jnp.where(match == owner.astype(F32), 0.5, 0.0)
        for g in range(3):
            for u, value in enumerate(probabilities(last[2 * g, at, :], matrix, ones, plan)):
                cols = slice((g * group + 2 * u) * LANES, (g * group + 2 * u + 2) * LANES)
                part[:, cols] = part[:, cols] - weight * value.astype(BF16).astype(F32)
        return carry

    if plan.n_peer == 2:
        other(0, 0)
    else:
        lax.fori_loop(0, plan.n_peer - 1, other, 0)

    wide = group * LANES
    dlog[...] = part[...].astype(BF16)
    level = one_xs
    for g in range(3):
        back = lax.dot_general(
            dlog[:, g * wide : (g + 1) * wide], own_matrix, (((1,), (1,)), ((), ())), preferred_element_type=F32
        )
        value = jnp.where(crop_mask(g, layers, base, plan), back * slope(pres[layers - 1, g]), 0.0)
        level[2 * g, at, :] = value.astype(BF16)
    product = lax.dot_general(
        hidden, dlog[:, wide : 2 * wide], (((0,), (0,)), ((), ())), preferred_element_type=F32
    )
    head_grad = jnp.zeros((ch, LANES), F32)
    for v in range(own):
        head_grad = head_grad + product[v * ch : (v + 1) * ch, v * LANES : (v + 1) * LANES]
    if not plan.spare:
        low = layers * plan.lane_blocks * ch
        grads[low : low + ch, :] = head_grad
    if plan.n * plan.chunk > plan.grad_rows:
        grads[plan.grad_rows :, :] = jnp.zeros((plan.n * plan.chunk - plan.grad_rows, LANES), F32)

    row = lax.rem(lax.broadcasted_iota(jnp.int32, (m, 1), 0), rows)
    wide_lane = lax.broadcasted_iota(jnp.int32, (1, PAIR), 1)
    for layer in reversed(range(layers)):
        u = plan.halo - layer - 1
        place = lax.rem(lane // ch - u % group + group, group)
        center = level[2 * (u // group), at, :].astype(F32)
        if u % group:
            center = jnp.where(lane // ch >= u % group, center, level[2 * (u // group) + 2, at, :].astype(F32))
        if own < group:
            center = jnp.where(place < own, center, 0.0)
        shifted = [
            jnp.where(row == rows - 1, 0.0, pltpu.roll(center, m - 1, 0)),
            center,
            jnp.where(row == 0, 0.0, pltpu.roll(center, 1, 0)),
        ]
        turned = jnp.concatenate([x.T.astype(BF16) for x in shifted], axis=0)
        slabs[0, at, :] = acts[layer, :, 0:LANES]
        slabs[1, at, :] = acts[layer, :, LANES:PAIR]
        blocks = [jnp.zeros((ch, PAIR), F32) for unused in range(round_up(plan.lane_blocks, 2) // 2)]
        for i in range(3):
            rhs = jnp.concatenate([slabs[n, i * rows : i * rows + m, :] for n in range(2)], axis=1)
            product = jnp.dot(turned, rhs, preferred_element_type=F32)
            for j in range(3):
                target = (3 * i + j) * 3 * ch
                total = None
                for b in range(own):
                    shift = (target - ((plan.halo + b - 1 - layer - group) % (2 * group)) * ch) % PAIR
                    low = j * LANES + ((u + b) % group) * ch
                    piece = product[low : low + ch]
                    piece = pltpu.roll(piece, shift, 1) if shift else piece
                    total = piece if total is None else total + piece
                for q in range(target // PAIR, (target + 3 * ch - 1) // PAIR + 1):
                    spot = wide_lane + q * PAIR
                    blocks[q] = jnp.where((spot >= target) & (spot < target + 3 * ch), total, blocks[q])
        for q in range(plan.lane_blocks):
            low = (layer * plan.lane_blocks + q) * ch
            block = blocks[q // 2][:, (q % 2) * LANES : (q % 2 + 1) * LANES]
            if plan.spare and q == plan.lane_blocks - 1:
                moved = pltpu.roll(head_grad, (LANES - plan.spare - layer * plan.spare) % LANES, 1)
                block = jnp.where(lane < LANES - plan.spare, block, moved)
            grads[low : low + ch, :] = block
        start = 2 * (layers - layer)
        target = two_xs if level is one_xs else one_xs
        fill_odd(level, [t for t in range(start // 2 - 1, plan.top // 2 - 1) if t % 2], plan)
        for b in range(start // group, plan.top_blocks):
            slots = (2 * b - 1 if b * group >= start else None, 2 * b)
            inside = crop_mask(b, layer, base, plan)

            def use(total, chunk, layer=layer, b=b, inside=inside, target=target):
                if layer > 0:
                    value = jnp.where(inside, total * slope(pres[layer - 1, b, chunk, :]), 0.0)
                    target[2 * b, rows + chunk.start : rows + chunk.stop, :] = value.astype(BF16)
                else:
                    result[chunk, :] = total

            convolve(level, slots, lambda half: back_band[0, layer, half], plan, use)
        level = target

    for d in range(plan.n_depth):
        for r in range(plan.n_row):
            p = d * plan.n_row + r
            parts = [grads[p * plan.chunk : (p + 1) * plan.chunk, :]]
            for k in range(plan.slab_depth):
                low = (d * plan.slab_depth + k) * rows + r * plan.slab_rows
                parts.append(result[low : low + plan.slab_rows])
            spare = plan.back_rows - plan.chunk - plan.slab
            if spare:
                parts.append(jnp.zeros((spare, LANES), F32))
            out_ref[p] = jnp.concatenate(parts, axis=0).astype(BF16)


def slope(pre):
    value = pre.astype(F32)
    sigma = 1.0 / (1.0 + jnp.exp(-value))
    return sigma * (1.0 + value * (1.0 - sigma))


def sum_kernel(plan, recv_ref, out_ref, back_ref):
    total = None
    backs = []
    for p in range(plan.n):
        value = recv_ref[p].astype(F32)
        part = value[0 : plan.chunk]
        total = part if total is None else total + part
        backs.append(value[plan.chunk : plan.chunk + plan.slab])
    total = total.astype(BF16)
    for p in range(plan.n):
        out_ref[p] = total
    lanes = plan.own * plan.channels
    step = LANES // lanes
    for q in range(plan.n // step):
        pieces = [backs[q * step + u][:, 0:lanes] for u in range(step)]
        piece = pieces[0] if step == 1 else jnp.concatenate(pieces, axis=1)
        for k in range(plan.slab_depth):
            rows = piece[k * plan.slab_rows : (k + 1) * plan.slab_rows]
            back_ref[k, :, q * LANES : (q + 1) * LANES] = rows.astype(BF16)


def unpack_kernel(plan, recv_ref, conv_ref, head_ref):
    ch = plan.channels
    flat = jnp.concatenate([recv_ref[p].astype(F32) for p in range(plan.n)], axis=0)
    lane = lax.broadcasted_iota(jnp.int32, (1, LANES), 1)
    head = flat[plan.layers * plan.lane_blocks * ch :][0:ch] if not plan.spare else jnp.zeros((ch, LANES), F32)
    for layer in range(plan.layers):
        for q in range(plan.lane_blocks):
            at = (layer * plan.lane_blocks + q) * ch
            count = min(LANES, plan.taps - q * LANES)
            block = flat[at : at + ch]
            conv_ref[0, layer, :, q * LANES : q * LANES + count] = block[:, 0:count]
            if plan.spare and q == plan.lane_blocks - 1:
                moved = pltpu.roll(block, (plan.spare + layer * plan.spare) % LANES, 1)
                head = jnp.where((lane >= layer * plan.spare) & (lane < (layer + 1) * plan.spare), moved, head)
    head_ref[0] = head[:, 0 : plan.classes]


def hbm(array):
    return pltpu.with_memory_space_constraint(array, pltpu.HBM)


def call(kernel, plan, out_shape, scratch=(), specs=(True,), cost=None, limit=16):
    vmem = pl.BlockSpec(memory_space=pltpu.VMEM)
    anywhere = pl.BlockSpec(memory_space=pl.ANY)
    many = isinstance(out_shape, (list, tuple))
    return pl.pallas_call(
        functools.partial(kernel, plan),
        out_shape=out_shape,
        in_specs=[vmem if x else anywhere for x in specs],
        out_specs=[vmem] * len(out_shape) if many else vmem,
        scratch_shapes=list(scratch),
        compiler_params=pltpu.CompilerParams(vmem_limit_bytes=limit * 1024 * 1024),
        cost_estimate=cost,
    )


def make_bands(plan, turned, backward):
    peers = turned.shape[0]
    shape = jax.ShapeDtypeStruct((peers, plan.layers, 3, 3 * LANES, LANES), BF16)
    made = call(
        lambda plan, *refs: band_kernel(plan, peers, backward, *refs),
        plan,
        [shape] * (2 if backward else 1),
        [
            pltpu.VMEM((plan.layers, plan.taps, PAIR), BF16),
            pltpu.VMEM((plan.layers, plan.taps // plan.channels, plan.channels, PAIR), BF16),
        ],
        cost=pl.CostEstimate(flops=10**9, bytes_accessed=4 * 10**6, transcendentals=0),
    )(turned)
    return made


def from_others(array, peers):
    moved = [lax.ppermute(array, "peer", [(i, (i + q) % peers) for i in range(peers)]) for q in range(1, peers)]
    return moved[0] if len(moved) == 1 else jnp.concatenate(moved, axis=0)


def body(mesh, features, labels, conv_weights, head_weights, matching):
    plan = Plan(mesh, features, labels, conv_weights, head_weights)
    shape = jax.ShapeDtypeStruct
    m, ch, n, layers = plan.m, plan.channels, plan.n, plan.layers
    head = jnp.pad(head_weights, ((0, 0), (0, 0), (0, LANES - plan.classes)))
    chunk_rows = plan.blocks * plan.slab + plan.slab_rows
    packed = call(
        pack_kernel,
        plan,
        shape((n, chunk_rows, LANES), BF16),
        [
            pltpu.SMEM(matching.shape[::-1], jnp.int32),
            pltpu.VMEM(features.shape, BF16),
            pltpu.VMEM(labels.shape, jnp.int32),
            pltpu.SemaphoreType.DMA((3,)),
        ],
        specs=(False,) * 3,
    )(hbm(matching.T), hbm(features), hbm(labels))
    slabs = lax.all_to_all(packed, GROUP, 0, 0, tiled=True)
    turned = jnp.swapaxes(conv_weights, 2, 3)
    others = from_others(turned, plan.n_peer)
    heads = from_others(head, plan.n_peer)
    band, back_band = make_bands(plan, turned, True)
    (other_band,) = make_bands(plan, others, False)
    padded = m + 2 * plan.rows
    wide = 3 * plan.group * LANES
    windows = 2 * plan.blocks
    parts = call(
        main_kernel,
        plan,
        shape((n, plan.back_rows, LANES), BF16),
        [
            pltpu.VMEM((windows, padded, LANES), BF16),
            pltpu.VMEM((windows, padded, LANES), BF16),
            pltpu.VMEM((windows, padded, LANES), BF16),
            pltpu.VMEM((layers, m, PAIR), BF16),
            pltpu.VMEM((layers, plan.top_blocks, m, LANES), BF16),
            pltpu.VMEM((m, LANES), F32),
            pltpu.VMEM((m, wide), F32),
            pltpu.VMEM((m, wide), BF16),
            pltpu.VMEM((n * plan.chunk, LANES), F32),
            pltpu.VMEM((m, LANES), F32),
        ],
        specs=(True,) * 6,
        limit=MAIN_MIB,
    )(slabs, band, back_band, other_band, head[0], heads)
    parts = lax.all_to_all(parts, GROUP, 0, 0, tiled=True)
    sums, input_grads = call(
        sum_kernel,
        plan,
        [shape((n, plan.chunk, LANES), BF16), shape(features.shape, BF16)],
    )(parts)
    sums = lax.all_to_all(sums, GROUP, 0, 0, tiled=True)
    conv_grads, head_grads = call(
        unpack_kernel,
        plan,
        [shape((1, layers, ch, plan.taps), F32), shape((1, ch, plan.classes), F32)],
    )(sums)
    return jnp.swapaxes(conv_grads, 2, 3), head_grads, input_grads[None]


def solution(mesh):
    placed = (
        P("depth", "row", None),
        P("depth", "row", None),
        P("peer", None, None, None),
        P("peer", None, None),
        P("depth", None),
    )
    return jax.shard_map(
        functools.partial(body, mesh),
        mesh=mesh,
        in_specs=placed,
        out_specs=(
            P("peer", None, None, None),
            P("peer", None, None),
            P("peer", "depth", "row", None),
        ),
        check_vma=False,
    )
```

```python
import functools

import jax
import jax.numpy as jnp
from jax import lax
from jax.experimental import pallas as pl
from jax.experimental.pallas import tpu as pltpu
from jax.sharding import PartitionSpec as P

LANES = 128
PAIR = 2 * LANES
F32 = jnp.float32
BF16 = jnp.bfloat16
GROUP = ("depth", "row")
FORWARD_MIB = 32
BACKWARD_MIB = 24
CHUNKS = 3


def round_up(value, step):
    return -(-value // step) * step


class Plan:
    def __init__(self, mesh, features, labels, conv_weights, head_weights):
        self.n_depth = mesh.shape["depth"]
        self.n_row = mesh.shape["row"]
        self.n_peer = mesh.shape["peer"]
        self.n = self.n_depth * self.n_row
        self.slab_depth, self.slab_rows, merged = features.shape
        self.layers, self.taps, self.channels = conv_weights.shape[1:]
        self.classes = head_weights.shape[2]
        self.width = merged // self.channels
        self.depth = self.slab_depth * self.n_depth
        self.rows = self.slab_rows * self.n_row
        self.m = self.depth * self.rows
        self.slab = self.slab_depth * self.slab_rows
        self.own = self.width // self.n
        self.group = LANES // self.channels
        self.halo = 2 * self.layers
        self.blocks = round_up(2 * self.halo + self.own, self.group) // self.group
        self.window = self.blocks * self.group
        self.top = self.window - 2 * self.layers
        self.top_blocks = round_up(self.top, self.group) // self.group
        self.lane_blocks = round_up(self.taps, LANES) // LANES
        spare = self.lane_blocks * LANES - self.taps
        self.spare = spare if spare * self.layers >= self.classes else 0
        self.grad_rows = (self.layers * self.lane_blocks + (0 if self.spare else 1)) * self.channels
        self.chunk = round_up(-(-self.grad_rows // self.n), 8)
        self.back_rows = round_up(self.chunk + self.slab, 8)


def crop_mask(block, level, base, plan):
    place = base + block * plan.group + level + lax.broadcasted_iota(jnp.int32, (1, LANES), 1) // plan.channels
    return (place >= 0) & (place < plan.width)


def first_half():
    return lax.broadcasted_iota(jnp.int32, (1, LANES), 1) < LANES // 2


def position(plan):
    return lax.axis_index("depth") * plan.n_row + lax.axis_index("row")


def clear_edges(xs, plan):
    rows = plan.rows
    zero = jnp.zeros((rows, LANES), BF16)
    for slot in range(xs.shape[0]):
        xs[slot, 0:rows, :] = zero
        xs[slot, rows + plan.m : 2 * rows + plan.m, :] = zero


def fill_odd(xs, slots, plan):
    at = slice(plan.rows, plan.rows + plan.m)
    for t in slots:
        xs[t, at, :] = jnp.where(first_half(), xs[t + 1, at, :], xs[t - 1, at, :])


def convolve(xs, slots, matrix, plan, use):
    rows = plan.rows
    mask = first_half()
    step = plan.m // CHUNKS
    row = lax.rem(lax.broadcasted_iota(jnp.int32, (step, 1), 0), rows)
    for c in range(CHUNKS):
        parts = []
        for half, slot in enumerate(slots):
            if slot is None:
                parts.append(None)
                continue
            low = c * step
            lhs = jnp.concatenate([xs[slot, i * rows + low : i * rows + low + step, :] for i in range(3)], axis=1)
            rhs = jnp.concatenate([matrix(half), matrix(2)], axis=1)
            parts.append(jnp.dot(lhs, rhs, preferred_element_type=F32))
        left = parts[0] if parts[0] is not None else parts[1]
        right = parts[1] if parts[1] is not None else parts[0]
        center = jnp.where(mask, left[:, :LANES], right[:, :LANES])
        before = pltpu.roll(jnp.where(mask, right[:, :LANES], left[:, :LANES]), LANES // 2, 1)
        after = jnp.where(mask, left[:, LANES:], right[:, LANES:])
        before = jnp.where(row == 0, 0.0, pltpu.roll(before, 1, 0))
        after = jnp.where(row == rows - 1, 0.0, pltpu.roll(after, step - 1, 0))
        use(before + center + after, slice(c * step, c * step + step))


SLOTS = ({1: 0, 0: 2, 2: 4}, {0: 0, 1: 2, 2: 6})


def lane_masks(plan):
    place = lax.broadcasted_iota(jnp.int32, (plan.channels, PAIR), 1) // plan.channels
    return [(place == q).astype(BF16) for q in range(PAIR // plan.channels)]


def band_rows(term, forward, i, p, half, masks):
    turned = (half == 1) if forward else (half == 0)
    f = (p - 2) % 4 if turned else p
    total = None
    for o in range(2):
        k = f - o if forward else o + 2 - f
        if not 0 <= k <= 2:
            continue
        for j in range(3):
            ij = 3 * i + j if forward else 3 * (2 - i) + 2 - j
            piece = term(3 * ij + k) * masks[SLOTS[half][j] + o]
            total = piece if total is None else total + piece
    return total


def band_kernel(plan, peers, backward, turned_ref, *refs):
    ch, group = plan.channels, plan.group
    outs, (wide, tall) = refs[:-2], refs[-2:]
    eye_r = lax.broadcasted_iota(jnp.int32, (ch, PAIR), 0)
    eye_l = lax.broadcasted_iota(jnp.int32, (ch, PAIR), 1)
    spread = (eye_r == lax.rem(eye_l, ch)).astype(BF16)
    zero = jnp.zeros_like(spread)
    spreads = jnp.concatenate(
        [jnp.concatenate([spread if u == v else zero for u in range(group)], axis=1) for v in range(group)], axis=0
    )
    masks = lane_masks(plan)
    for peer in range(peers):
        for layer in range(plan.layers):
            weights = turned_ref[peer, layer]
            wide[layer] = lax.dot_general(
                weights, spread, (((0,), (0,)), ((), ())), preferred_element_type=F32
            ).astype(BF16)
            for q in range(plan.lane_blocks if backward else 0):
                count = min(LANES, plan.taps - q * LANES)
                part = jnp.dot(
                    weights[:, q * LANES : q * LANES + count], spreads[0:count], preferred_element_type=F32
                ).astype(BF16)
                for u in range(count // ch):
                    tall[layer, q * group + u] = part[:, u * PAIR : (u + 1) * PAIR]

        def one(layer, carry, peer=peer):
            for out, ahead, term in (
                (outs[0], True, lambda n: wide[layer, n * ch : (n + 1) * ch, :]),
                (outs[-1], False, lambda n: tall[layer, n]),
            )[: len(outs)]:
                for i in range(3):
                    for p in range(group):
                        at = slice((i * group + p) * ch, (i * group + p + 1) * ch)
                        first, second = [band_rows(term, ahead, i, p, half, masks) for half in range(2)]
                        out[peer, layer, 0, at, :] = first[:, :LANES]
                        out[peer, layer, 1, at, :] = second[:, :LANES]
                        out[peer, layer, 2, at, :] = first[:, LANES:] + second[:, LANES:]
            return carry

        lax.fori_loop(0, plan.layers, one, 0)


def head_matrix(head, plan):
    ch, group = plan.channels, plan.group
    lanes = lax.broadcasted_iota(jnp.int32, (ch, group * LANES), 1) // LANES
    wide = jnp.concatenate([head] * group, axis=1)
    zero = jnp.zeros_like(wide)
    return jnp.concatenate([jnp.where(lanes == v, wide, zero) for v in range(group)], axis=0)


def pack_kernel(plan, match_hbm, feat_hbm, label_hbm, out_ref, match_ref, feat_ref, label_ref, sems):
    ch, own = plan.channels, plan.own
    copies = [
        pltpu.make_async_copy(source, target, sems.at[n])
        for n, (source, target) in enumerate(((feat_hbm, feat_ref), (label_hbm, label_ref), (match_hbm, match_ref)))
    ]
    for copy in copies:
        copy.start()
    for copy in copies:
        copy.wait()
    feats = feat_ref[...].astype(F32).reshape(plan.slab, plan.width * ch)
    labels = label_ref[...].astype(F32)
    peer = lax.axis_index("peer")
    lane = lax.broadcasted_iota(jnp.int32, (plan.slab_rows, LANES), 1)
    seen = 3 * plan.group
    matches = jnp.zeros((plan.slab_rows, LANES), F32)
    for k in range(plan.slab_depth):
        matches = jnp.where(lane == LANES - plan.slab_depth + k, match_ref[peer, k].astype(F32), matches)

    def cut(array, low, high, limit):
        pieces = []
        if low < 0:
            pieces.append(jnp.zeros((array.shape[0], min(-low, high - low)), F32))
        if max(low, 0) < min(high, limit):
            pieces.append(array[:, max(low, 0) : min(high, limit)])
        if high > limit:
            pieces.append(jnp.zeros((array.shape[0], min(high - limit, high - low)), F32))
        return jnp.concatenate(pieces, axis=1) if len(pieces) > 1 else pieces[0]

    for p in range(plan.n):
        first = p * own - plan.halo
        parts = []
        for q in range(plan.blocks):
            low = (first + q * plan.group) * ch
            parts.append(cut(feats, low, low + LANES, plan.width * ch))
        low = p * own + plan.layers - plan.halo
        pieces = []
        for k in range(plan.slab_depth):
            pieces.append(cut(labels[k], low, low + seen, plan.width))
        pieces.append(jnp.zeros((plan.slab_rows, LANES - plan.slab_depth * seen), F32))
        parts.append(jnp.concatenate(pieces, axis=1) + matches)
        out_ref[p] = jnp.concatenate(parts, axis=0).astype(BF16)


def unpack_slabs(plan, recv_ref, source, label_ref):
    rows = plan.rows
    lane = lax.broadcasted_iota(jnp.int32, (1, LANES), 1)
    seen = 3 * plan.group
    keep = LANES - plan.slab_depth
    for d in range(plan.n_depth):
        parts = [recv_ref[d * plan.n_row + r].astype(F32) for r in range(plan.n_row)]
        for k in range(plan.slab_depth):
            at = (d * plan.slab_depth + k) * rows
            for q in range(plan.blocks + 1):
                low = q * plan.slab + k * plan.slab_rows if q < plan.blocks else plan.blocks * plan.slab
                piece = jnp.concatenate([x[low : low + plan.slab_rows] for x in parts], axis=0)
                if q < plan.blocks:
                    source[2 * q, rows + at : rows + at + rows, :] = piece.astype(BF16)
                    continue
                if k > 0:
                    moved = pltpu.roll(piece, LANES - k * seen, 1)
                    piece = jnp.where(lane < seen, moved, pltpu.roll(piece, LANES - k, 1))
                label_ref[at : at + rows, :] = jnp.where((lane < seen) | (lane == keep), piece, 0.0)


def forward_steps(plan, buffers, matrix, base, keep):
    m, rows, group = plan.m, plan.rows, plan.group
    at = slice(rows, rows + m)
    count = plan.window
    source = buffers[0]
    for layer in range(plan.layers):
        target = buffers[1 + layer % 2]
        fill_odd(source, range(1, (count - 4) // 2 + 1, 2), plan)
        keep(layer, source)
        count -= 2
        for b in range(round_up(count, group) // group):
            slots = (2 * b, 2 * b + 1 if b * group + 2 < count else None)
            inside = crop_mask(b, layer + 1, base, plan)

            def use(total, part, layer=layer, b=b, inside=inside, target=target):
                keep(layer, None, b, total, part)
                value = total / (1.0 + jnp.exp(-total))
                target[2 * b, rows + part.start : rows + part.stop, :] = jnp.where(inside, value, 0.0).astype(BF16)

            convolve(source, slots, lambda half: matrix(layer, half), plan, use)
            yield
        source = target


def last_of(buffers, plan):
    return buffers[1 + (plan.layers - 1) % 2]


def class_ones(plan):
    rows = lax.broadcasted_iota(jnp.int32, (2 * LANES, 2 * LANES), 0)
    lanes = lax.broadcasted_iota(jnp.int32, (2 * LANES, 2 * LANES), 1)
    return (rows // LANES == lanes // LANES).astype(BF16)


def probabilities(act, matrix, ones, plan):
    logits = jnp.dot(act, matrix, preferred_element_type=F32)
    lane = lax.rem(lax.broadcasted_iota(jnp.int32, (1, 2 * LANES), 1), LANES)
    probs = []
    for v in range(0, plan.group, 2):
        exponent = jnp.where(lane < plan.classes, jnp.exp(logits[:, v * LANES : (v + 2) * LANES]), 0.0)
        high = exponent.astype(BF16)
        rest = (exponent - high.astype(F32)).astype(BF16)
        total = jnp.dot(high, ones, preferred_element_type=F32) + jnp.dot(rest, ones, preferred_element_type=F32)
        probs.append(exponent / total)
    return probs


def forward_kernel(plan, recv_ref, band, other_band, head_ref, heads_ref, acts, pres, dlog, hidden_ref, *scratch):
    slabs, one_xs, two_xs, three_xs, four_xs, label_ref, part = scratch
    m, rows, group = plan.m, plan.rows, plan.group
    base = position(plan) * plan.own - plan.halo
    peer = lax.axis_index("peer")
    buffers, others = (slabs, one_xs, two_xs), (slabs, three_xs, four_xs)
    for xs in scratch[:5]:
        clear_edges(xs, plan)
    unpack_slabs(plan, recv_ref, slabs, label_ref)
    at = slice(rows, rows + m)
    half_mask = first_half()

    def drop(*unused):
        pass

    def keep(layer, source, b=None, total=None, part=None):
        if source is not None:
            if layer == 0:
                acts[0, :, 0:LANES] = jnp.where(half_mask, source[6, at, :], source[2, at, :])
            else:
                acts[layer, :, 0:LANES] = source[2, at, :]
            acts[layer, :, LANES:PAIR] = source[4, at, :]
        elif b < plan.top_blocks:
            pres[layer, b, part, :] = total.astype(BF16)

    own_steps = forward_steps(plan, buffers, lambda layer, half: band[0, layer, half], base, keep)
    if plan.n_peer == 2:
        other_steps = forward_steps(plan, others, lambda layer, half: other_band[0, layer, half], base, drop)
        for unused in zip(own_steps, other_steps):
            pass
        for unused in other_steps:
            pass
    else:
        for unused in own_steps:
            pass
    last = last_of(buffers, plan)
    own_matrix = head_matrix(head_ref[...], plan)
    ones = class_ones(plan)
    pair_lane = lax.rem(lax.broadcasted_iota(jnp.int32, (1, PAIR), 1), LANES).astype(F32)
    spread_r = lax.broadcasted_iota(jnp.int32, (LANES, PAIR), 0)
    spread_l = lax.broadcasted_iota(jnp.int32, (LANES, PAIR), 1) // LANES
    labels = label_ref[...]
    codes = labels.astype(BF16)
    match = labels[:, LANES - plan.slab_depth : LANES - plan.slab_depth + 1]
    weight = jnp.where(match == peer.astype(F32), 0.5, 0.0)
    def minus_targets(g, u, value):
        place = g * group + 2 * u
        spread = (spread_r == spread_l + place).astype(BF16)
        label = jnp.dot(codes, spread, preferred_element_type=F32)
        onehot = jnp.where(label == pair_lane, 0.5, 0.0)
        return value - onehot - weight * value.astype(BF16).astype(F32)

    def columns_of(g, u):
        return slice((g * group + 2 * u) * LANES, (g * group + 2 * u + 2) * LANES)

    def other_share(q, last):
        owner = lax.rem(peer - q - 1 + plan.n_peer, plan.n_peer)
        matrix = head_matrix(heads_ref[q], plan)
        weight = jnp.where(match == owner.astype(F32), 0.5, 0.0)
        for g in range(3):
            for u, value in enumerate(probabilities(last[2 * g, at, :], matrix, ones, plan)):
                yield g, u, weight * value.astype(BF16).astype(F32)

    own_probs = (
        (g, u, value)
        for g in range(3)
        for u, value in enumerate(probabilities(last[2 * g, at, :], own_matrix, ones, plan))
    )
    if plan.n_peer == 2:
        for (g, u, value), (unused, unused, share) in zip(own_probs, other_share(0, last_of(others, plan))):
            dlog[:, columns_of(g, u)] = (minus_targets(g, u, value) - share).astype(BF16)
    else:
        for g, u, value in own_probs:
            part[:, columns_of(g, u)] = minus_targets(g, u, value)
    hidden_ref[...] = last[2, at, :]

    def other(q, carry):
        for unused in forward_steps(plan, others, lambda layer, half: other_band[q, layer, half], base, drop):
            pass
        for g, u, share in other_share(q, last_of(others, plan)):
            part[:, columns_of(g, u)] = part[:, columns_of(g, u)] - share
        return carry

    if plan.n_peer > 2:
        lax.fori_loop(0, plan.n_peer - 1, other, 0)
        dlog[...] = part[...].astype(BF16)


def backward_kernel(plan, back_band, head_ref, acts, pres, dlog, hidden_ref, out_ref, *scratch):
    slabs, one_xs, two_xs, grads, result = scratch
    ch, m, rows, group, own, layers = plan.channels, plan.m, plan.rows, plan.group, plan.own, plan.layers
    base = position(plan) * own - plan.halo
    for xs in scratch[:3]:
        clear_edges(xs, plan)
    at = slice(rows, rows + m)
    lane = lax.broadcasted_iota(jnp.int32, (1, LANES), 1)
    own_matrix = head_matrix(head_ref[...], plan)
    hidden = hidden_ref[...]

    wide = group * LANES
    level = one_xs
    for g in range(3):
        back = lax.dot_general(
            dlog[:, g * wide : (g + 1) * wide], own_matrix, (((1,), (1,)), ((), ())), preferred_element_type=F32
        )
        value = jnp.where(crop_mask(g, layers, base, plan), back * slope(pres[layers - 1, g]), 0.0)
        level[2 * g, at, :] = value.astype(BF16)
    product = lax.dot_general(
        hidden, dlog[:, wide : 2 * wide], (((0,), (0,)), ((), ())), preferred_element_type=F32
    )
    head_grad = jnp.zeros((ch, LANES), F32)
    for v in range(own):
        head_grad = head_grad + product[v * ch : (v + 1) * ch, v * LANES : (v + 1) * LANES]
    if not plan.spare:
        low = layers * plan.lane_blocks * ch
        grads[low : low + ch, :] = head_grad
    if plan.n * plan.chunk > plan.grad_rows:
        grads[plan.grad_rows :, :] = jnp.zeros((plan.n * plan.chunk - plan.grad_rows, LANES), F32)

    row = lax.rem(lax.broadcasted_iota(jnp.int32, (m, 1), 0), rows)
    wide_lane = lax.broadcasted_iota(jnp.int32, (1, PAIR), 1)
    for layer in reversed(range(layers)):
        u = plan.halo - layer - 1
        place = lax.rem(lane // ch - u % group + group, group)
        center = level[2 * (u // group), at, :].astype(F32)
        if u % group:
            center = jnp.where(lane // ch >= u % group, center, level[2 * (u // group) + 2, at, :].astype(F32))
        if own < group:
            center = jnp.where(place < own, center, 0.0)
        shifted = [
            jnp.where(row == rows - 1, 0.0, pltpu.roll(center, m - 1, 0)),
            center,
            jnp.where(row == 0, 0.0, pltpu.roll(center, 1, 0)),
        ]
        turned = jnp.concatenate([x.T.astype(BF16) for x in shifted], axis=0)
        slabs[0, at, :] = acts[layer, :, 0:LANES]
        slabs[1, at, :] = acts[layer, :, LANES:PAIR]
        blocks = [jnp.zeros((ch, PAIR), F32) for unused in range(round_up(plan.lane_blocks, 2) // 2)]
        for i in range(3):
            rhs = jnp.concatenate([slabs[n, i * rows : i * rows + m, :] for n in range(2)], axis=1)
            product = jnp.dot(turned, rhs, preferred_element_type=F32)
            for j in range(3):
                target = (3 * i + j) * 3 * ch
                total = None
                for b in range(own):
                    shift = (target - ((plan.halo + b - 1 - layer - group) % (2 * group)) * ch) % PAIR
                    low = j * LANES + ((u + b) % group) * ch
                    piece = product[low : low + ch]
                    piece = pltpu.roll(piece, shift, 1) if shift else piece
                    total = piece if total is None else total + piece
                for q in range(target // PAIR, (target + 3 * ch - 1) // PAIR + 1):
                    spot = wide_lane + q * PAIR
                    blocks[q] = jnp.where((spot >= target) & (spot < target + 3 * ch), total, blocks[q])
        for q in range(plan.lane_blocks):
            low = (layer * plan.lane_blocks + q) * ch
            block = blocks[q // 2][:, (q % 2) * LANES : (q % 2 + 1) * LANES]
            if plan.spare and q == plan.lane_blocks - 1:
                moved = pltpu.roll(head_grad, (LANES - plan.spare - layer * plan.spare) % LANES, 1)
                block = jnp.where(lane < LANES - plan.spare, block, moved)
            grads[low : low + ch, :] = block
        start = 2 * (layers - layer)
        target = two_xs if level is one_xs else one_xs
        fill_odd(level, [t for t in range(start // 2 - 1, plan.top // 2 - 1) if t % 2], plan)
        for b in range(start // group, plan.top_blocks):
            slots = (2 * b - 1 if b * group >= start else None, 2 * b)
            inside = crop_mask(b, layer, base, plan)

            def use(total, chunk, layer=layer, b=b, inside=inside, target=target):
                if layer > 0:
                    value = jnp.where(inside, total * slope(pres[layer - 1, b, chunk, :]), 0.0)
                    target[2 * b, rows + chunk.start : rows + chunk.stop, :] = value.astype(BF16)
                else:
                    result[chunk, :] = total

            convolve(level, slots, lambda half: back_band[0, layer, half], plan, use)
        level = target

    for d in range(plan.n_depth):
        for r in range(plan.n_row):
            p = d * plan.n_row + r
            parts = [grads[p * plan.chunk : (p + 1) * plan.chunk, :]]
            for k in range(plan.slab_depth):
                low = (d * plan.slab_depth + k) * rows + r * plan.slab_rows
                parts.append(result[low : low + plan.slab_rows])
            spare = plan.back_rows - plan.chunk - plan.slab
            if spare:
                parts.append(jnp.zeros((spare, LANES), F32))
            out_ref[p] = jnp.concatenate(parts, axis=0).astype(BF16)


def slope(pre):
    value = pre.astype(F32)
    sigma = 1.0 / (1.0 + jnp.exp(-value))
    return sigma * (1.0 + value * (1.0 - sigma))


def sum_kernel(plan, recv_ref, out_ref, back_ref):
    total = None
    backs = []
    for p in range(plan.n):
        value = recv_ref[p].astype(F32)
        part = value[0 : plan.chunk]
        total = part if total is None else total + part
        backs.append(value[plan.chunk : plan.chunk + plan.slab])
    total = total.astype(BF16)
    for p in range(plan.n):
        out_ref[p] = total
    lanes = plan.own * plan.channels
    step = LANES // lanes
    for q in range(plan.n // step):
        pieces = [backs[q * step + u][:, 0:lanes] for u in range(step)]
        piece = pieces[0] if step == 1 else jnp.concatenate(pieces, axis=1)
        for k in range(plan.slab_depth):
            rows = piece[k * plan.slab_rows : (k + 1) * plan.slab_rows]
            back_ref[k, :, q * LANES : (q + 1) * LANES] = rows.astype(BF16)


def unpack_kernel(plan, recv_ref, conv_ref, head_ref):
    ch = plan.channels
    flat = jnp.concatenate([recv_ref[p].astype(F32) for p in range(plan.n)], axis=0)
    lane = lax.broadcasted_iota(jnp.int32, (1, LANES), 1)
    head = flat[plan.layers * plan.lane_blocks * ch :][0:ch] if not plan.spare else jnp.zeros((ch, LANES), F32)
    for layer in range(plan.layers):
        for q in range(plan.lane_blocks):
            at = (layer * plan.lane_blocks + q) * ch
            count = min(LANES, plan.taps - q * LANES)
            block = flat[at : at + ch]
            conv_ref[0, layer, :, q * LANES : q * LANES + count] = block[:, 0:count]
            if plan.spare and q == plan.lane_blocks - 1:
                moved = pltpu.roll(block, (plan.spare + layer * plan.spare) % LANES, 1)
                head = jnp.where((lane >= layer * plan.spare) & (lane < (layer + 1) * plan.spare), moved, head)
    head_ref[0] = head[:, 0 : plan.classes]


def hbm(array):
    return pltpu.with_memory_space_constraint(array, pltpu.HBM)


def call(kernel, plan, out_shape, scratch=(), specs=(True,), cost=None, limit=16):
    vmem = pl.BlockSpec(memory_space=pltpu.VMEM)
    anywhere = pl.BlockSpec(memory_space=pl.ANY)
    many = isinstance(out_shape, (list, tuple))
    return pl.pallas_call(
        functools.partial(kernel, plan),
        out_shape=out_shape,
        in_specs=[vmem if x else anywhere for x in specs],
        out_specs=[vmem] * len(out_shape) if many else vmem,
        scratch_shapes=list(scratch),
        compiler_params=pltpu.CompilerParams(vmem_limit_bytes=limit * 1024 * 1024),
        cost_estimate=cost,
    )


def make_bands(plan, turned, backward):
    peers = turned.shape[0]
    shape = jax.ShapeDtypeStruct((peers, plan.layers, 3, 3 * LANES, LANES), BF16)
    made = call(
        lambda plan, *refs: band_kernel(plan, peers, backward, *refs),
        plan,
        [shape, pltpu.HBM(shape.shape, shape.dtype)] if backward else [shape],
        [
            pltpu.VMEM((plan.layers, plan.taps, PAIR), BF16),
            pltpu.VMEM((plan.layers, plan.taps // plan.channels, plan.channels, PAIR), BF16),
        ],
        cost=pl.CostEstimate(flops=10**9, bytes_accessed=4 * 10**6, transcendentals=0),
    )(turned)
    return made


def from_others(array, peers):
    moved = [lax.ppermute(array, "peer", [(i, (i + q) % peers) for i in range(peers)]) for q in range(1, peers)]
    return moved[0] if len(moved) == 1 else jnp.concatenate(moved, axis=0)


def body(mesh, features, labels, conv_weights, head_weights, matching):
    plan = Plan(mesh, features, labels, conv_weights, head_weights)
    shape = jax.ShapeDtypeStruct
    m, ch, n, layers = plan.m, plan.channels, plan.n, plan.layers
    head = jnp.pad(head_weights, ((0, 0), (0, 0), (0, LANES - plan.classes)))
    chunk_rows = plan.blocks * plan.slab + plan.slab_rows
    packed = call(
        pack_kernel,
        plan,
        shape((n, chunk_rows, LANES), BF16),
        [
            pltpu.SMEM(matching.shape[::-1], jnp.int32),
            pltpu.VMEM(features.shape, BF16),
            pltpu.VMEM(labels.shape, jnp.int32),
            pltpu.SemaphoreType.DMA((3,)),
        ],
        specs=(False,) * 3,
    )(hbm(matching.T), hbm(features), hbm(labels))
    slabs = lax.all_to_all(packed, GROUP, 0, 0, tiled=True)
    turned = jnp.swapaxes(conv_weights, 2, 3)
    others = from_others(turned, plan.n_peer)
    heads = from_others(head, plan.n_peer)
    band, back_band = make_bands(plan, turned, True)
    (other_band,) = make_bands(plan, others, False)
    padded = m + 2 * plan.rows
    wide = 3 * plan.group * LANES
    windows = 2 * plan.blocks
    kept = call(
        forward_kernel,
        plan,
        [
            shape((layers, m, PAIR), BF16),
            shape((layers, plan.top_blocks, m, LANES), BF16),
            shape((m, wide), BF16),
            shape((m, LANES), BF16),
        ],
        [pltpu.VMEM((windows, padded, LANES), BF16)] * 5
        + [
            pltpu.VMEM((m, LANES), F32),
            pltpu.VMEM((m, wide), F32),
        ],
        specs=(True,) * 5,
        cost=pl.CostEstimate(flops=8 * 10**9, bytes_accessed=10**7, transcendentals=0),
        limit=FORWARD_MIB,
    )(slabs, band, other_band, head[0], heads)
    parts = call(
        backward_kernel,
        plan,
        shape((n, plan.back_rows, LANES), BF16),
        [
            pltpu.VMEM((2, padded, LANES), BF16),
            pltpu.VMEM((2 * plan.top_blocks, padded, LANES), BF16),
            pltpu.VMEM((2 * plan.top_blocks, padded, LANES), BF16),
            pltpu.VMEM((n * plan.chunk, LANES), F32),
            pltpu.VMEM((m, LANES), F32),
        ],
        specs=(True,) * 6,
        limit=BACKWARD_MIB,
    )(back_band, head[0], *kept)
    parts = lax.all_to_all(parts, GROUP, 0, 0, tiled=True)
    sums, input_grads = call(
        sum_kernel,
        plan,
        [shape((n, plan.chunk, LANES), BF16), shape(features.shape, BF16)],
    )(parts)
    sums = lax.all_to_all(sums, GROUP, 0, 0, tiled=True)
    conv_grads, head_grads = call(
        unpack_kernel,
        plan,
        [shape((1, layers, ch, plan.taps), F32), shape((1, ch, plan.classes), F32)],
    )(sums)
    return jnp.swapaxes(conv_grads, 2, 3), head_grads, input_grads[None]


def solution(mesh):
    placed = (
        P("depth", "row", None),
        P("depth", "row", None),
        P("peer", None, None, None),
        P("peer", None, None),
        P("depth", None),
    )
    return jax.shard_map(
        functools.partial(body, mesh),
        mesh=mesh,
        in_specs=placed,
        out_specs=(
            P("peer", None, None, None),
            P("peer", None, None),
            P("peer", "depth", "row", None),
        ),
        check_vma=False,
    )
```

```python
import functools

import jax
import jax.numpy as jnp
from jax import lax
from jax.experimental import pallas as pl
from jax.experimental.pallas import tpu as pltpu
from jax.sharding import PartitionSpec as P

LANES = 128
PAIR = 2 * LANES
F32 = jnp.float32
BF16 = jnp.bfloat16
GROUP = ("depth", "row")
FORWARD_MIB = 32
BACKWARD_MIB = 24
CHUNKS = 3
BACK_CHUNKS = 2


def round_up(value, step):
    return -(-value // step) * step


class Plan:
    def __init__(self, mesh, features, labels, conv_weights, head_weights):
        self.n_depth = mesh.shape["depth"]
        self.n_row = mesh.shape["row"]
        self.n_peer = mesh.shape["peer"]
        self.n = self.n_depth * self.n_row
        self.slab_depth, self.slab_rows, merged = features.shape
        self.layers, self.taps, self.channels = conv_weights.shape[1:]
        self.classes = head_weights.shape[2]
        self.width = merged // self.channels
        self.depth = self.slab_depth * self.n_depth
        self.rows = self.slab_rows * self.n_row
        self.m = self.depth * self.rows
        self.slab = self.slab_depth * self.slab_rows
        self.own = self.width // self.n
        self.group = LANES // self.channels
        self.halo = 2 * self.layers
        self.blocks = round_up(2 * self.halo + self.own, self.group) // self.group
        self.window = self.blocks * self.group
        self.top = self.window - 2 * self.layers
        self.top_blocks = round_up(self.top, self.group) // self.group
        self.lane_blocks = round_up(self.taps, LANES) // LANES
        spare = self.lane_blocks * LANES - self.taps
        self.spare = spare if spare * self.layers >= self.classes else 0
        self.grad_rows = (self.layers * self.lane_blocks + (0 if self.spare else 1)) * self.channels
        self.chunk = round_up(-(-self.grad_rows // self.n), 8)
        self.back_rows = round_up(self.chunk + self.slab, 8)


def crop_mask(block, level, base, plan):
    place = base + block * plan.group + level + lax.broadcasted_iota(jnp.int32, (1, LANES), 1) // plan.channels
    return (place >= 0) & (place < plan.width)


def first_half():
    return lax.broadcasted_iota(jnp.int32, (1, LANES), 1) < LANES // 2


def position(plan):
    return lax.axis_index("depth") * plan.n_row + lax.axis_index("row")


def clear_edges(xs, plan):
    rows = plan.rows
    zero = jnp.zeros((rows, LANES), BF16)
    for slot in range(xs.shape[0]):
        xs[slot, 0:rows, :] = zero
        xs[slot, rows + plan.m : 2 * rows + plan.m, :] = zero


def fill_odd(xs, slots, plan):
    at = slice(plan.rows, plan.rows + plan.m)
    for t in slots:
        xs[t, at, :] = jnp.where(first_half(), xs[t + 1, at, :], xs[t - 1, at, :])


def convolve(xs, slots, matrix, plan, use, chunks=CHUNKS):
    rows = plan.rows
    mask = first_half()
    step = plan.m // chunks
    row = lax.rem(lax.broadcasted_iota(jnp.int32, (step, 1), 0), rows)
    for c in range(chunks):
        parts = []
        for half, slot in enumerate(slots):
            if slot is None:
                parts.append(None)
                continue
            low = c * step
            lhs = jnp.concatenate([xs[slot, i * rows + low : i * rows + low + step, :] for i in range(3)], axis=1)
            rhs = jnp.concatenate([matrix(half), matrix(2)], axis=1)
            parts.append(jnp.dot(lhs, rhs, preferred_element_type=F32))
        left = parts[0] if parts[0] is not None else parts[1]
        right = parts[1] if parts[1] is not None else parts[0]
        center = jnp.where(mask, left[:, :LANES], right[:, :LANES])
        before = pltpu.roll(jnp.where(mask, right[:, :LANES], left[:, :LANES]), LANES // 2, 1)
        after = jnp.where(mask, left[:, LANES:], right[:, LANES:])
        before = jnp.where(row == 0, 0.0, pltpu.roll(before, 1, 0))
        after = jnp.where(row == rows - 1, 0.0, pltpu.roll(after, step - 1, 0))
        use(before + center + after, slice(c * step, c * step + step))


SLOTS = ({1: 0, 0: 2, 2: 4}, {0: 0, 1: 2, 2: 6})


def lane_masks(plan):
    place = lax.broadcasted_iota(jnp.int32, (plan.channels, PAIR), 1) // plan.channels
    return [(place == q).astype(BF16) for q in range(PAIR // plan.channels)]


def band_rows(term, forward, i, p, half, masks):
    turned = (half == 1) if forward else (half == 0)
    f = (p - 2) % 4 if turned else p
    total = None
    for o in range(2):
        k = f - o if forward else o + 2 - f
        if not 0 <= k <= 2:
            continue
        for j in range(3):
            ij = 3 * i + j if forward else 3 * (2 - i) + 2 - j
            piece = term(3 * ij + k) * masks[SLOTS[half][j] + o]
            total = piece if total is None else total + piece
    return total


def band_kernel(plan, peers, backward, turned_ref, *refs):
    ch, group = plan.channels, plan.group
    outs, (wide, tall) = refs[:-2], refs[-2:]
    eye_r = lax.broadcasted_iota(jnp.int32, (ch, PAIR), 0)
    eye_l = lax.broadcasted_iota(jnp.int32, (ch, PAIR), 1)
    spread = (eye_r == lax.rem(eye_l, ch)).astype(BF16)
    zero = jnp.zeros_like(spread)
    spreads = jnp.concatenate(
        [jnp.concatenate([spread if u == v else zero for u in range(group)], axis=1) for v in range(group)], axis=0
    )
    masks = lane_masks(plan)
    for peer in range(peers):
        for layer in range(plan.layers):
            weights = turned_ref[peer, layer]
            wide[layer] = lax.dot_general(
                weights, spread, (((0,), (0,)), ((), ())), preferred_element_type=F32
            ).astype(BF16)
            for q in range(plan.lane_blocks if backward else 0):
                count = min(LANES, plan.taps - q * LANES)
                part = jnp.dot(
                    weights[:, q * LANES : q * LANES + count], spreads[0:count], preferred_element_type=F32
                ).astype(BF16)
                for u in range(count // ch):
                    tall[layer, q * group + u] = part[:, u * PAIR : (u + 1) * PAIR]

        def one(layer, carry, peer=peer):
            for out, ahead, term in (
                (outs[0], True, lambda n: wide[layer, n * ch : (n + 1) * ch, :]),
                (outs[-1], False, lambda n: tall[layer, n]),
            )[: len(outs)]:
                for i in range(3):
                    for p in range(group):
                        at = slice((i * group + p) * ch, (i * group + p + 1) * ch)
                        first, second = [band_rows(term, ahead, i, p, half, masks) for half in range(2)]
                        out[peer, layer, 0, at, :] = first[:, :LANES]
                        out[peer, layer, 1, at, :] = second[:, :LANES]
                        out[peer, layer, 2, at, :] = first[:, LANES:] + second[:, LANES:]
            return carry

        lax.fori_loop(0, plan.layers, one, 0)


def head_matrix(head, plan):
    ch, group = plan.channels, plan.group
    lanes = lax.broadcasted_iota(jnp.int32, (ch, group * LANES), 1) // LANES
    wide = jnp.concatenate([head] * group, axis=1)
    zero = jnp.zeros_like(wide)
    return jnp.concatenate([jnp.where(lanes == v, wide, zero) for v in range(group)], axis=0)


def pack_kernel(plan, match_hbm, feat_hbm, label_hbm, out_ref, match_ref, feat_ref, label_ref, sems):
    ch, own = plan.channels, plan.own
    copies = [
        pltpu.make_async_copy(source, target, sems.at[n])
        for n, (source, target) in enumerate(((feat_hbm, feat_ref), (label_hbm, label_ref), (match_hbm, match_ref)))
    ]
    for copy in copies:
        copy.start()
    for copy in copies:
        copy.wait()
    feats = feat_ref[...].astype(F32).reshape(plan.slab, plan.width * ch)
    labels = label_ref[...].astype(F32)
    peer = lax.axis_index("peer")
    lane = lax.broadcasted_iota(jnp.int32, (plan.slab_rows, LANES), 1)
    seen = 3 * plan.group
    matches = jnp.zeros((plan.slab_rows, LANES), F32)
    for k in range(plan.slab_depth):
        matches = jnp.where(lane == LANES - plan.slab_depth + k, match_ref[peer, k].astype(F32), matches)

    def cut(array, low, high, limit):
        pieces = []
        if low < 0:
            pieces.append(jnp.zeros((array.shape[0], min(-low, high - low)), F32))
        if max(low, 0) < min(high, limit):
            pieces.append(array[:, max(low, 0) : min(high, limit)])
        if high > limit:
            pieces.append(jnp.zeros((array.shape[0], min(high - limit, high - low)), F32))
        return jnp.concatenate(pieces, axis=1) if len(pieces) > 1 else pieces[0]

    for p in range(plan.n):
        first = p * own - plan.halo
        parts = []
        for q in range(plan.blocks):
            low = (first + q * plan.group) * ch
            parts.append(cut(feats, low, low + LANES, plan.width * ch))
        low = p * own + plan.layers - plan.halo
        pieces = []
        for k in range(plan.slab_depth):
            pieces.append(cut(labels[k], low, low + seen, plan.width))
        pieces.append(jnp.zeros((plan.slab_rows, LANES - plan.slab_depth * seen), F32))
        parts.append(jnp.concatenate(pieces, axis=1) + matches)
        out_ref[p] = jnp.concatenate(parts, axis=0).astype(BF16)


def unpack_slabs(plan, recv_ref, source, label_ref):
    rows = plan.rows
    lane = lax.broadcasted_iota(jnp.int32, (1, LANES), 1)
    seen = 3 * plan.group
    keep = LANES - plan.slab_depth
    for d in range(plan.n_depth):
        parts = [recv_ref[d * plan.n_row + r].astype(F32) for r in range(plan.n_row)]
        for k in range(plan.slab_depth):
            at = (d * plan.slab_depth + k) * rows
            for q in range(plan.blocks + 1):
                low = q * plan.slab + k * plan.slab_rows if q < plan.blocks else plan.blocks * plan.slab
                piece = jnp.concatenate([x[low : low + plan.slab_rows] for x in parts], axis=0)
                if q < plan.blocks:
                    source[2 * q, rows + at : rows + at + rows, :] = piece.astype(BF16)
                    continue
                if k > 0:
                    moved = pltpu.roll(piece, LANES - k * seen, 1)
                    piece = jnp.where(lane < seen, moved, pltpu.roll(piece, LANES - k, 1))
                label_ref[at : at + rows, :] = jnp.where((lane < seen) | (lane == keep), piece, 0.0)


def forward_steps(plan, buffers, matrix, base, keep, filled=False):
    m, rows, group = plan.m, plan.rows, plan.group
    at = slice(rows, rows + m)
    count = plan.window
    source = buffers[0]
    for layer in range(plan.layers):
        target = buffers[1 + layer % 2]
        if layer > 0 or not filled:
            fill_odd(source, range(1, (count - 4) // 2 + 1, 2), plan)
        keep(layer, source)
        count -= 2
        for b in range(round_up(count, group) // group):
            slots = (2 * b, 2 * b + 1 if b * group + 2 < count else None)
            inside = crop_mask(b, layer + 1, base, plan)

            def use(total, part, layer=layer, b=b, inside=inside, target=target):
                keep(layer, None, b, total, part)
                value = total / (1.0 + jnp.exp(-total))
                target[2 * b, rows + part.start : rows + part.stop, :] = jnp.where(inside, value, 0.0).astype(BF16)

            convolve(source, slots, lambda half: matrix(layer, half), plan, use)
            yield
        source = target


def last_of(buffers, plan):
    return buffers[1 + (plan.layers - 1) % 2]


def class_ones(plan):
    rows = lax.broadcasted_iota(jnp.int32, (2 * LANES, 2 * LANES), 0)
    lanes = lax.broadcasted_iota(jnp.int32, (2 * LANES, 2 * LANES), 1)
    return (rows // LANES == lanes // LANES).astype(BF16)


def probabilities(act, matrix, ones, plan):
    logits = jnp.dot(act, matrix, preferred_element_type=F32)
    lane = lax.rem(lax.broadcasted_iota(jnp.int32, (1, 2 * LANES), 1), LANES)
    probs = []
    for v in range(0, plan.group, 2):
        exponent = jnp.where(lane < plan.classes, jnp.exp(logits[:, v * LANES : (v + 2) * LANES]), 0.0)
        high = exponent.astype(BF16)
        rest = (exponent - high.astype(F32)).astype(BF16)
        total = jnp.dot(high, ones, preferred_element_type=F32) + jnp.dot(rest, ones, preferred_element_type=F32)
        probs.append(exponent / total)
    return probs


def forward_kernel(plan, recv_ref, band, other_band, head_ref, heads_ref, acts, pres, dlog, hidden_ref, *scratch):
    slabs, one_xs, two_xs, three_xs, four_xs, label_ref, part = scratch
    m, rows, group = plan.m, plan.rows, plan.group
    base = position(plan) * plan.own - plan.halo
    peer = lax.axis_index("peer")
    buffers, others = (slabs, one_xs, two_xs), (slabs, three_xs, four_xs)
    for xs in scratch[:5]:
        clear_edges(xs, plan)
    unpack_slabs(plan, recv_ref, slabs, label_ref)
    at = slice(rows, rows + m)
    half_mask = first_half()

    def drop(*unused):
        pass

    def keep(layer, source, b=None, total=None, part=None):
        if source is not None:
            if layer == 0:
                acts[0, :, 0:LANES] = jnp.where(half_mask, source[6, at, :], source[2, at, :])
            else:
                acts[layer, :, 0:LANES] = source[2, at, :]
            acts[layer, :, LANES:PAIR] = source[4, at, :]
        elif b < plan.top_blocks:
            pres[layer, b, part, :] = total.astype(BF16)

    own_steps = forward_steps(plan, buffers, lambda layer, half: band[0, layer, half], base, keep)
    if plan.n_peer == 2:
        other_steps = forward_steps(plan, others, lambda layer, half: other_band[0, layer, half], base, drop, True)
        for unused in zip(own_steps, other_steps):
            pass
        for unused in other_steps:
            pass
    else:
        for unused in own_steps:
            pass
    last = last_of(buffers, plan)
    own_matrix = head_matrix(head_ref[...], plan)
    ones = class_ones(plan)
    pair_lane = lax.rem(lax.broadcasted_iota(jnp.int32, (1, PAIR), 1), LANES).astype(F32)
    spread_r = lax.broadcasted_iota(jnp.int32, (LANES, PAIR), 0)
    spread_l = lax.broadcasted_iota(jnp.int32, (LANES, PAIR), 1) // LANES
    labels = label_ref[...]
    codes = labels.astype(BF16)
    match = labels[:, LANES - plan.slab_depth : LANES - plan.slab_depth + 1]
    weight = jnp.where(match == peer.astype(F32), 0.5, 0.0)
    def minus_targets(g, u, value):
        place = g * group + 2 * u
        spread = (spread_r == spread_l + place).astype(BF16)
        label = jnp.dot(codes, spread, preferred_element_type=F32)
        onehot = jnp.where(label == pair_lane, 0.5, 0.0)
        return value - onehot - weight * value.astype(BF16).astype(F32)

    def columns_of(g, u):
        return slice((g * group + 2 * u) * LANES, (g * group + 2 * u + 2) * LANES)

    def other_share(q, last):
        owner = lax.rem(peer - q - 1 + plan.n_peer, plan.n_peer)
        matrix = head_matrix(heads_ref[q], plan)
        weight = jnp.where(match == owner.astype(F32), 0.5, 0.0)
        for g in range(3):
            for u, value in enumerate(probabilities(last[2 * g, at, :], matrix, ones, plan)):
                yield g, u, weight * value.astype(BF16).astype(F32)

    own_probs = (
        (g, u, value)
        for g in range(3)
        for u, value in enumerate(probabilities(last[2 * g, at, :], own_matrix, ones, plan))
    )
    if plan.n_peer == 2:
        for (g, u, value), (unused, unused, share) in zip(own_probs, other_share(0, last_of(others, plan))):
            dlog[:, columns_of(g, u)] = (minus_targets(g, u, value) - share).astype(BF16)
    else:
        for g, u, value in own_probs:
            part[:, columns_of(g, u)] = minus_targets(g, u, value)
    hidden_ref[...] = last[2, at, :]

    def other(q, carry):
        for unused in forward_steps(plan, others, lambda layer, half: other_band[q, layer, half], base, drop, True):
            pass
        for g, u, share in other_share(q, last_of(others, plan)):
            part[:, columns_of(g, u)] = part[:, columns_of(g, u)] - share
        return carry

    if plan.n_peer > 2:
        lax.fori_loop(0, plan.n_peer - 1, other, 0)
        dlog[...] = part[...].astype(BF16)


def backward_kernel(plan, back_band, head_ref, acts, pres, dlog, hidden_ref, out_ref, *scratch):
    slabs, one_xs, two_xs, grads, result = scratch
    ch, m, rows, group, own, layers = plan.channels, plan.m, plan.rows, plan.group, plan.own, plan.layers
    base = position(plan) * own - plan.halo
    for xs in scratch[:3]:
        clear_edges(xs, plan)
    at = slice(rows, rows + m)
    lane = lax.broadcasted_iota(jnp.int32, (1, LANES), 1)
    own_matrix = head_matrix(head_ref[...], plan)
    hidden = hidden_ref[...]

    wide = group * LANES
    level = one_xs
    for g in range(3):
        back = lax.dot_general(
            dlog[:, g * wide : (g + 1) * wide], own_matrix, (((1,), (1,)), ((), ())), preferred_element_type=F32
        )
        value = jnp.where(crop_mask(g, layers, base, plan), back * slope(pres[layers - 1, g]), 0.0)
        level[2 * g, at, :] = value.astype(BF16)
    product = lax.dot_general(
        hidden, dlog[:, wide : 2 * wide], (((0,), (0,)), ((), ())), preferred_element_type=F32
    )
    head_grad = jnp.zeros((ch, LANES), F32)
    for v in range(own):
        head_grad = head_grad + product[v * ch : (v + 1) * ch, v * LANES : (v + 1) * LANES]
    if not plan.spare:
        low = layers * plan.lane_blocks * ch
        grads[low : low + ch, :] = head_grad
    if plan.n * plan.chunk > plan.grad_rows:
        grads[plan.grad_rows :, :] = jnp.zeros((plan.n * plan.chunk - plan.grad_rows, LANES), F32)

    row = lax.rem(lax.broadcasted_iota(jnp.int32, (m, 1), 0), rows)
    wide_lane = lax.broadcasted_iota(jnp.int32, (1, PAIR), 1)
    for layer in reversed(range(layers)):
        u = plan.halo - layer - 1
        place = lax.rem(lane // ch - u % group + group, group)
        center = level[2 * (u // group), at, :].astype(F32)
        if u % group:
            center = jnp.where(lane // ch >= u % group, center, level[2 * (u // group) + 2, at, :].astype(F32))
        if own < group:
            center = jnp.where(place < own, center, 0.0)
        shifted = [
            jnp.where(row == rows - 1, 0.0, pltpu.roll(center, m - 1, 0)),
            center,
            jnp.where(row == 0, 0.0, pltpu.roll(center, 1, 0)),
        ]
        turned = jnp.concatenate([x.T.astype(BF16) for x in shifted], axis=0)
        slabs[0, at, :] = acts[layer, :, 0:LANES]
        slabs[1, at, :] = acts[layer, :, LANES:PAIR]
        blocks = [jnp.zeros((ch, PAIR), F32) for unused in range(round_up(plan.lane_blocks, 2) // 2)]
        for i in range(3):
            rhs = jnp.concatenate([slabs[n, i * rows : i * rows + m, :] for n in range(2)], axis=1)
            product = jnp.dot(turned, rhs, preferred_element_type=F32)
            for j in range(3):
                target = (3 * i + j) * 3 * ch
                total = None
                for b in range(own):
                    shift = (target - ((plan.halo + b - 1 - layer - group) % (2 * group)) * ch) % PAIR
                    low = j * LANES + ((u + b) % group) * ch
                    piece = product[low : low + ch]
                    piece = pltpu.roll(piece, shift, 1) if shift else piece
                    total = piece if total is None else total + piece
                for q in range(target // PAIR, (target + 3 * ch - 1) // PAIR + 1):
                    spot = wide_lane + q * PAIR
                    blocks[q] = jnp.where((spot >= target) & (spot < target + 3 * ch), total, blocks[q])
        for q in range(plan.lane_blocks):
            low = (layer * plan.lane_blocks + q) * ch
            block = blocks[q // 2][:, (q % 2) * LANES : (q % 2 + 1) * LANES]
            if plan.spare and q == plan.lane_blocks - 1:
                moved = pltpu.roll(head_grad, (LANES - plan.spare - layer * plan.spare) % LANES, 1)
                block = jnp.where(lane < LANES - plan.spare, block, moved)
            grads[low : low + ch, :] = block
        start = 2 * (layers - layer)
        target = two_xs if level is one_xs else one_xs
        fill_odd(level, [t for t in range(start // 2 - 1, plan.top // 2 - 1) if t % 2], plan)
        for b in range(start // group, plan.top_blocks):
            slots = (2 * b - 1 if b * group >= start else None, 2 * b)
            inside = crop_mask(b, layer, base, plan)

            def use(total, chunk, layer=layer, b=b, inside=inside, target=target):
                if layer > 0:
                    value = jnp.where(inside, total * slope(pres[layer - 1, b, chunk, :]), 0.0)
                    target[2 * b, rows + chunk.start : rows + chunk.stop, :] = value.astype(BF16)
                else:
                    result[chunk, :] = total

            convolve(level, slots, lambda half: back_band[0, layer, half], plan, use, BACK_CHUNKS)
        level = target

    for d in range(plan.n_depth):
        for r in range(plan.n_row):
            p = d * plan.n_row + r
            parts = [grads[p * plan.chunk : (p + 1) * plan.chunk, :]]
            for k in range(plan.slab_depth):
                low = (d * plan.slab_depth + k) * rows + r * plan.slab_rows
                parts.append(result[low : low + plan.slab_rows])
            spare = plan.back_rows - plan.chunk - plan.slab
            if spare:
                parts.append(jnp.zeros((spare, LANES), F32))
            out_ref[p] = jnp.concatenate(parts, axis=0).astype(BF16)


def slope(pre):
    value = pre.astype(F32)
    sigma = 1.0 / (1.0 + jnp.exp(-value))
    return sigma * (1.0 + value * (1.0 - sigma))


def sum_kernel(plan, recv_ref, out_ref, back_ref):
    total = None
    backs = []
    for p in range(plan.n):
        value = recv_ref[p].astype(F32)
        part = value[0 : plan.chunk]
        total = part if total is None else total + part
        backs.append(value[plan.chunk : plan.chunk + plan.slab])
    total = total.astype(BF16)
    for p in range(plan.n):
        out_ref[p] = total
    lanes = plan.own * plan.channels
    step = LANES // lanes
    for q in range(plan.n // step):
        pieces = [backs[q * step + u][:, 0:lanes] for u in range(step)]
        piece = pieces[0] if step == 1 else jnp.concatenate(pieces, axis=1)
        for k in range(plan.slab_depth):
            rows = piece[k * plan.slab_rows : (k + 1) * plan.slab_rows]
            back_ref[k, :, q * LANES : (q + 1) * LANES] = rows.astype(BF16)


def unpack_kernel(plan, recv_ref, conv_ref, head_ref):
    ch = plan.channels
    flat = jnp.concatenate([recv_ref[p].astype(F32) for p in range(plan.n)], axis=0)
    lane = lax.broadcasted_iota(jnp.int32, (1, LANES), 1)
    head = flat[plan.layers * plan.lane_blocks * ch :][0:ch] if not plan.spare else jnp.zeros((ch, LANES), F32)
    for layer in range(plan.layers):
        for q in range(plan.lane_blocks):
            at = (layer * plan.lane_blocks + q) * ch
            count = min(LANES, plan.taps - q * LANES)
            block = flat[at : at + ch]
            conv_ref[0, layer, :, q * LANES : q * LANES + count] = block[:, 0:count]
            if plan.spare and q == plan.lane_blocks - 1:
                moved = pltpu.roll(block, (plan.spare + layer * plan.spare) % LANES, 1)
                head = jnp.where((lane >= layer * plan.spare) & (lane < (layer + 1) * plan.spare), moved, head)
    head_ref[0] = head[:, 0 : plan.classes]


def hbm(array):
    return pltpu.with_memory_space_constraint(array, pltpu.HBM)


def call(kernel, plan, out_shape, scratch=(), specs=(True,), cost=None, limit=16):
    vmem = pl.BlockSpec(memory_space=pltpu.VMEM)
    anywhere = pl.BlockSpec(memory_space=pl.ANY)
    many = isinstance(out_shape, (list, tuple))
    return pl.pallas_call(
        functools.partial(kernel, plan),
        out_shape=out_shape,
        in_specs=[vmem if x else anywhere for x in specs],
        out_specs=[vmem] * len(out_shape) if many else vmem,
        scratch_shapes=list(scratch),
        compiler_params=pltpu.CompilerParams(vmem_limit_bytes=limit * 1024 * 1024),
        cost_estimate=cost,
    )


def make_bands(plan, turned, backward):
    peers = turned.shape[0]
    shape = jax.ShapeDtypeStruct((peers, plan.layers, 3, 3 * LANES, LANES), BF16)
    made = call(
        lambda plan, *refs: band_kernel(plan, peers, backward, *refs),
        plan,
        [shape, pltpu.HBM(shape.shape, shape.dtype)] if backward else [shape],
        [
            pltpu.VMEM((plan.layers, plan.taps, PAIR), BF16),
            pltpu.VMEM((plan.layers, plan.taps // plan.channels, plan.channels, PAIR), BF16),
        ],
        cost=pl.CostEstimate(flops=10**9, bytes_accessed=4 * 10**6, transcendentals=0),
    )(turned)
    return made


def from_others(array, peers):
    moved = [lax.ppermute(array, "peer", [(i, (i + q) % peers) for i in range(peers)]) for q in range(1, peers)]
    return moved[0] if len(moved) == 1 else jnp.concatenate(moved, axis=0)


def body(mesh, features, labels, conv_weights, head_weights, matching):
    plan = Plan(mesh, features, labels, conv_weights, head_weights)
    shape = jax.ShapeDtypeStruct
    m, ch, n, layers = plan.m, plan.channels, plan.n, plan.layers
    head = jnp.pad(head_weights, ((0, 0), (0, 0), (0, LANES - plan.classes)))
    chunk_rows = plan.blocks * plan.slab + plan.slab_rows
    packed = call(
        pack_kernel,
        plan,
        shape((n, chunk_rows, LANES), BF16),
        [
            pltpu.SMEM(matching.shape[::-1], jnp.int32),
            pltpu.VMEM(features.shape, BF16),
            pltpu.VMEM(labels.shape, jnp.int32),
            pltpu.SemaphoreType.DMA((3,)),
        ],
        specs=(False,) * 3,
    )(hbm(matching.T), hbm(features), hbm(labels))
    slabs = lax.all_to_all(packed, GROUP, 0, 0, tiled=True)
    turned = jnp.swapaxes(conv_weights, 2, 3)
    others = from_others(turned, plan.n_peer)
    heads = from_others(head, plan.n_peer)
    band, back_band = make_bands(plan, turned, True)
    (other_band,) = make_bands(plan, others, False)
    padded = m + 2 * plan.rows
    wide = 3 * plan.group * LANES
    windows = 2 * plan.blocks
    kept = call(
        forward_kernel,
        plan,
        [
            shape((layers, m, PAIR), BF16),
            shape((layers, plan.top_blocks, m, LANES), BF16),
            shape((m, wide), BF16),
            shape((m, LANES), BF16),
        ],
        [pltpu.VMEM((windows, padded, LANES), BF16)] * 5
        + [
            pltpu.VMEM((m, LANES), F32),
            pltpu.VMEM((m, wide), F32),
        ],
        specs=(True,) * 5,
        cost=pl.CostEstimate(flops=8 * 10**9, bytes_accessed=10**7, transcendentals=0),
        limit=FORWARD_MIB,
    )(slabs, band, other_band, head[0], heads)
    parts = call(
        backward_kernel,
        plan,
        shape((n, plan.back_rows, LANES), BF16),
        [
            pltpu.VMEM((2, padded, LANES), BF16),
            pltpu.VMEM((2 * plan.top_blocks, padded, LANES), BF16),
            pltpu.VMEM((2 * plan.top_blocks, padded, LANES), BF16),
            pltpu.VMEM((n * plan.chunk, LANES), F32),
            pltpu.VMEM((m, LANES), F32),
        ],
        specs=(True,) * 6,
        limit=BACKWARD_MIB,
    )(back_band, head[0], *kept)
    parts = lax.all_to_all(parts, GROUP, 0, 0, tiled=True)
    sums, input_grads = call(
        sum_kernel,
        plan,
        [shape((n, plan.chunk, LANES), BF16), shape(features.shape, BF16)],
    )(parts)
    sums = lax.all_to_all(sums, GROUP, 0, 0, tiled=True)
    conv_grads, head_grads = call(
        unpack_kernel,
        plan,
        [shape((1, layers, ch, plan.taps), F32), shape((1, ch, plan.classes), F32)],
    )(sums)
    return jnp.swapaxes(conv_grads, 2, 3), head_grads, input_grads[None]


def solution(mesh):
    placed = (
        P("depth", "row", None),
        P("depth", "row", None),
        P("peer", None, None, None),
        P("peer", None, None),
        P("depth", None),
    )
    return jax.shard_map(
        functools.partial(body, mesh),
        mesh=mesh,
        in_specs=placed,
        out_specs=(
            P("peer", None, None, None),
            P("peer", None, None),
            P("peer", "depth", "row", None),
        ),
        check_vma=False,
    )
```
